256 devices in a mesh: seq: 32 (over x, z_hi, core), fsdp: 8 (over y, z_lo).
Axes of the slice: x: 4, y: 4, z: 8 (z_hi: 4, z_lo: 2; z = z_hi * 2 + z_lo), core: 2. Of those that a mesh axis runs over, the one named last changes fastest.
Arguments:
- block_in: bfloat16 [8, 32, 256, 1152], P('fsdp', 'seq'), may hold values from -6 to 6
- spatial_qkv: bfloat16 [8, 32, 256, 3456], P('fsdp', 'seq'), may hold values from -18 to 18
- cotangent: bfloat16 [8, 32, 256, 1152], P('fsdp', 'seq'), may hold values from -6 to 6
- w_sproj: bfloat16 [1152, 1152], P('fsdp'), may hold values from -0.1875 to 0.1875
- w_tqkv: bfloat16 [1152, 3456], P('fsdp'), may hold values from -8 to 8
- w_tproj: bfloat16 [1152, 1152], P('fsdp'), may hold values from -0.1875 to 0.1875
- t_gain: float32 [1152], replicated, may hold values from 0.25 to 1.75
Outputs:
- block_out: bfloat16 [8, 32, 256, 1152], P('fsdp', 'seq')
- grad_in: bfloat16 [8, 32, 256, 1152], P('fsdp', 'seq')
- grad_qkv: bfloat16 [8, 32, 256, 3456], P('fsdp', 'seq')
- grad_sproj: float32 [1152, 1152], P('fsdp', 'seq')
- grad_tproj: float32 [1152, 1152], P('fsdp', 'seq')
- grad_gain: float32 [1152], replicated
The draws below stay inside these ranges and needn't reach their ends.
All inputs are finite; a program needn't handle non-finite values.
Results may differ from the reference program's by a relative error of at most 0.035.
Values may be sent and summed in bfloat16 or wider, within the bound.
No kernel may reach another device: no remote copies, remote signals or barrier semaphores. Data moves between devices by JAX's collectives and lax.ppermute only.
A program may use at most 128 MiB of HBM per device.

```python
import math
import jax
import jax.numpy as jnp
from jax import lax

D = 1152
HEADS = 16
HD = 72
PATCHES = 256
FRAMES = 32
CLIPS = 8


def draw_spatial_qkv(key, part):
    key = jax.random.fold_in(key, 17)
    key_base = jax.random.fold_in(key, 0)
    draw_shape = (CLIPS, FRAMES, PATCHES, 3 * D)
    base_draw = jnp.clip(jax.random.normal(key_base, draw_shape, jnp.float32), -6.0, 6.0)
    return base_draw.astype(jnp.bfloat16)


def draw_w_tqkv(key, part):
    key = jax.random.fold_in(key, 29)
    key_base = jax.random.fold_in(key, 0)
    fan_scale = 1.0 / D ** 0.5
    weight = jnp.clip(jax.random.normal(key_base, (D, 3 * D), jnp.float32), -6.0, 6.0) * fan_scale
    weight = jnp.clip(weight, -8.0, 8.0)
    return weight.astype(jnp.bfloat16)


def levels(rng, dims, shards, least, top_value):
    level, own = 1.0, jax.random.fold_in(rng, 6)
    for dim, parts in shards:
        draws = jnp.exp(jax.random.uniform(jax.random.fold_in(own, dim), (parts,), jnp.float32, least / len(shards), top_value / len(shards)))
        level = level * jnp.repeat(draws, dims[dim] // parts).reshape([-1 if axis == dim else 1 for axis in range(len(dims))])
    return level


def noise(own_key, extent, spread, reach, cuts=(), held_as=jnp.bfloat16):
    gain = levels(own_key, extent, cuts, -0.22, 0.18) if cuts else 1.0
    values = jax.random.normal(own_key, extent, jnp.float32) * spread * gain
    return jnp.minimum(jnp.maximum(values, -reach), reach).astype(held_as)


def setup_inputs(seed: int = 0) -> dict:
    keys = jax.random.split(jax.random.key(seed), 8)
    return {
        "block_in": noise(keys[0], (CLIPS, FRAMES, PATCHES, D), 1.0, 6.0, ((0, 8), (1, 32))),
        "spatial_qkv": draw_spatial_qkv(jax.random.fold_in(keys[7], 71), 0),
        "cotangent": noise(keys[2], (CLIPS, FRAMES, PATCHES, D), 1.0, 6.0, ((0, 8), (1, 32))),
        "w_sproj": noise(keys[3], (D, D), D ** -0.5, 0.1875, ((0, 8),)),
        "w_tqkv": draw_w_tqkv(jax.random.fold_in(keys[7], 71), 0),
        "w_tproj": noise(keys[5], (D, D), D ** -0.5, 0.1875, ((0, 8),)),
        "t_gain": jnp.clip(1.0 + 0.15 * jax.random.normal(keys[6], (D,), jnp.float32), 0.25, 1.75),
    }


EPSILON = 1e-06
SPACE_FORMS = ('bqhe,bkhe->bhqk', 'bhqk,bkhe->bqhe', 'bhqk,bqhe->bkhe')
TIME_FORMS = ('cqphe,ckphe->cphqk', 'cphqk,ckphe->cqphe', 'cphqk,cqphe->ckphe')

def attend(queries, key_rows, values, score_scale, layout_forms):
    scores = jnp.einsum(layout_forms[0], queries.astype(jnp.float32), key_rows.astype(jnp.float32)) * score_scale
    attn_probs = jax.nn.softmax(scores, axis=-1)
    probs_low = attn_probs.astype(jnp.bfloat16).astype(jnp.float32)
    mixed_out = jnp.einsum(layout_forms[1], probs_low, values.astype(jnp.float32)).astype(jnp.bfloat16)
    return (mixed_out, attn_probs)

def attend_back(queries, key_rows, values, attn_probs, grad_out, score_scale, layout_forms):
    probs_low = attn_probs.astype(jnp.bfloat16).astype(jnp.float32)
    grad_wide = grad_out.astype(jnp.float32)
    grad_values = jnp.einsum(layout_forms[2], probs_low, grad_wide).astype(jnp.bfloat16)
    grad_probs = jnp.einsum(layout_forms[0], grad_wide, values.astype(jnp.float32))
    grad_scores = attn_probs * (grad_probs - lax.optimization_barrier(jnp.sum(attn_probs * grad_probs, axis=-1, keepdims=True)))
    scores_low = (grad_scores * score_scale).astype(jnp.bfloat16).astype(jnp.float32)
    grad_queries = jnp.einsum(layout_forms[1], scores_low, key_rows.astype(jnp.float32)).astype(jnp.bfloat16)
    grad_keys = jnp.einsum(layout_forms[2], scores_low, queries.astype(jnp.float32)).astype(jnp.bfloat16)
    return (grad_queries, grad_keys, grad_values)

def layer_stats(hidden_low, gain_vec):
    values_wide = hidden_low.astype(jnp.float32)
    centre = lax.optimization_barrier(jnp.mean(values_wide, axis=-1, keepdims=True))
    centred = values_wide - centre
    variance = lax.optimization_barrier(jnp.mean(centred * centred, axis=-1, keepdims=True))
    inv_dev = lax.rsqrt(variance + EPSILON)
    standard = centred * inv_dev
    normed_low = (standard * gain_vec.astype(jnp.float32)).astype(jnp.bfloat16)
    return (normed_low, standard, inv_dev)

def block_sum(left_rows, right_rows):

    def accumulate(running, group_pair):
        term = jnp.dot(group_pair[0].T, group_pair[1], preferred_element_type=jnp.float32)
        rounded = lax.optimization_barrier(term.astype(jnp.bfloat16))
        return (running + rounded.astype(jnp.float32), None)
    start = jnp.zeros((left_rows.shape[2], right_rows.shape[2]), jnp.float32)
    return lax.scan(accumulate, start, (left_rows, right_rows))[0]

def regroup(rows_array):
    block_len = PATCHES // FRAMES
    last_width = rows_array.shape[-1]
    split = rows_array.reshape(CLIPS, FRAMES, FRAMES, block_len, last_width)
    return split.transpose(0, 2, 1, 3, 4).reshape(CLIPS * FRAMES, FRAMES * block_len, last_width)

def reference(block_in, spatial_qkv, cotangent, w_sproj, w_tqkv, w_tproj, t_gain):
    score_scale = 1.0 / math.sqrt(HD)
    frame_qkv = spatial_qkv.reshape(CLIPS * FRAMES, PATCHES, 3, HEADS, HD)

    def space_forward(frame_block):
        mixed_out, ignored = attend(frame_block[None, :, 0], frame_block[None, :, 1], frame_block[None, :, 2], score_scale, SPACE_FORMS)
        return mixed_out[0]
    space_out = lax.map(space_forward, frame_qkv)
    space_flat = space_out.reshape(-1, D)
    hidden = block_in.reshape(-1, D).astype(jnp.float32) + jnp.dot(space_flat, w_sproj, preferred_element_type=jnp.float32)
    hidden_low = hidden.astype(jnp.bfloat16)
    normed_low, standard, inv_dev = layer_stats(hidden_low, t_gain)
    time_qkv = jnp.dot(normed_low, w_tqkv, preferred_element_type=jnp.float32).astype(jnp.bfloat16)
    time_qkv = time_qkv.reshape(CLIPS, FRAMES, PATCHES, 3, HEADS, HD)
    time_out, time_probs = attend(time_qkv[:, :, :, 0], time_qkv[:, :, :, 1], time_qkv[:, :, :, 2], score_scale, TIME_FORMS)
    time_flat = time_out.reshape(-1, D)
    result = hidden_low.astype(jnp.float32) + jnp.dot(time_flat, w_tproj, preferred_element_type=jnp.float32)
    block_out = result.astype(jnp.bfloat16).reshape(CLIPS, FRAMES, PATCHES, D)
    grad_rows = cotangent.reshape(-1, D)
    grad_time = jnp.dot(grad_rows, w_tproj.T, preferred_element_type=jnp.float32).astype(jnp.bfloat16)
    grad_time = grad_time.reshape(time_out.shape)
    time_grads = attend_back(time_qkv[:, :, :, 0], time_qkv[:, :, :, 1], time_qkv[:, :, :, 2], time_probs, grad_time, score_scale, TIME_FORMS)
    grad_time_qkv = jnp.stack(time_grads, axis=3).reshape(-1, 3 * D)
    grad_normed = jnp.dot(grad_time_qkv, w_tqkv.T, preferred_element_type=jnp.float32)
    scaled = grad_normed * t_gain.astype(jnp.float32)
    correction = scaled - lax.optimization_barrier(jnp.mean(scaled, axis=-1, keepdims=True)) - standard * lax.optimization_barrier(jnp.mean(scaled * standard, axis=-1, keepdims=True))
    grad_hidden = grad_rows.astype(jnp.float32) + correction * inv_dev
    grad_low = grad_hidden.astype(jnp.bfloat16)
    grad_gain = lax.optimization_barrier(jnp.sum(grad_normed * standard, axis=0))
    grad_space = jnp.dot(grad_low, w_sproj.T, preferred_element_type=jnp.float32).astype(jnp.bfloat16)
    grad_space = grad_space.reshape(space_out.shape)

    def space_backward(frame_pair):
        frame_block, grad_block = frame_pair
        queries = frame_block[None, :, 0]
        key_rows = frame_block[None, :, 1]
        values = frame_block[None, :, 2]
        ignored, attn_probs = attend(queries, key_rows, values, score_scale, SPACE_FORMS)
        space_grads = attend_back(queries, key_rows, values, attn_probs, grad_block[None], score_scale, SPACE_FORMS)
        return jnp.stack(space_grads, axis=2)[0]
    grad_qkv = lax.map(space_backward, (frame_qkv, grad_space)).reshape(CLIPS, FRAMES, PATCHES, 3 * D)
    grad_sproj = block_sum(space_flat.reshape(CLIPS * FRAMES, PATCHES, D), grad_low.reshape(CLIPS * FRAMES, PATCHES, D))
    grad_tproj = block_sum(regroup(time_flat.reshape(CLIPS, FRAMES, PATCHES, D)), regroup(cotangent))
    grad_in = grad_low.reshape(CLIPS, FRAMES, PATCHES, D)
    return (block_out, grad_in, grad_qkv, grad_sproj, grad_tproj, grad_gain)
```

```python
import functools
import math

import jax
import jax.numpy as jnp
from jax import lax
from jax.experimental import pallas as pl
from jax.experimental.pallas import tpu as pltpu
from jax.sharding import Mesh, PartitionSpec as P

HEADS = 16
HD = 72
D = 1152
TOK = 256
EPSILON = 1e-06
SCALE = 1.0 / math.sqrt(HD)
LOG2E = 1.4426950408889634
HALF_D = 640
HALF_QKV = 1792
BF = jnp.bfloat16
F32 = jnp.float32
FS = ("y", "zl")
SEQ = ("x", "zh", "core")
VMEM = pl.BlockSpec(memory_space=pltpu.VMEM)
NT = (((1,), (1,)), ((), ()))
TN = (((0,), (0,)), ((), ()))


def nn(a, b):
    return jnp.dot(a, b, preferred_element_type=F32)


def nt(a, b):
    return lax.dot_general(a, b, NT, preferred_element_type=F32)


def tn(a, b):
    return lax.dot_general(a, b, TN, preferred_element_type=F32)


def window(head):
    lo = HD * head // 128 * 128
    hi = -(-(HD * head + HD) // 128) * 128
    cols = lax.broadcasted_iota(jnp.int32, (TOK, hi - lo), 1)
    inside = (cols >= HD * head - lo) & (cols < HD * head + HD - lo)
    return lo, hi, inside


def keep(inside, block):
    return jnp.where(inside, block, jnp.zeros_like(block))


def same_patch():
    rows = lax.broadcasted_iota(jnp.int32, (TOK, TOK), 0)
    cols = lax.broadcasted_iota(jnp.int32, (TOK, TOK), 1)
    return (rows & 7) == (cols & 7)


def attend(qkv, probs, acc, temporal):
    acc[...] = jnp.zeros_like(acc)
    for head in range(HEADS):
        lo, hi, inside = window(head)
        q = qkv[:, lo:hi]
        k = keep(inside, qkv[:, D + lo : D + hi])
        v = keep(inside, qkv[:, 2 * D + lo : 2 * D + hi])
        s = nt(q, k) * (SCALE * LOG2E)
        if temporal:
            s = jnp.where(same_patch(), s, -jnp.inf)
        e = jnp.exp2(s - jnp.max(s, axis=-1, keepdims=True))
        p = (e * (1.0 / jnp.sum(e, axis=-1, keepdims=True))).astype(BF)
        probs[head] = p
        acc[:, lo:hi] += nn(p, v)


def attend_back(qkv, probs, grad, acc):
    acc[...] = jnp.zeros_like(acc)
    for head in range(HEADS):
        lo, hi, inside = window(head)
        q = keep(inside, qkv[:, lo:hi])
        k = keep(inside, qkv[:, D + lo : D + hi])
        v = qkv[:, 2 * D + lo : 2 * D + hi]
        g = keep(inside, grad[:, lo:hi])
        p_low = probs[head]
        p = p_low.astype(F32)
        dp = nt(g, v)
        t = p * dp
        ds = ((t - p * jnp.sum(t, axis=-1, keepdims=True)) * SCALE).astype(BF)
        acc[:, lo:hi] += nn(ds, k)
        acc[:, D + lo : D + hi] += tn(ds, q)
        acc[:, 2 * D + lo : 2 * D + hi] += tn(p_low, g)


def space_forward(qkv, mix, probs, acc):
    attend(qkv, probs, acc, False)
    mix[...] = acc[...].astype(BF)


def project(mix, w, residual, out):
    out[:, :HALF_D] = (residual[:, :HALF_D].astype(F32) + nn(mix[...], w[0])).astype(BF)
    out[:, HALF_D:] = (
        residual[:, HALF_D:].astype(F32) + nn(mix[...], w[1, :, 2 * HALF_D - D :])
    ).astype(BF)


def back_project(grad, w):
    return nt(grad[:, :HALF_D], w[0]) + nt(grad[:, HALF_D:], w[1, :, 2 * HALF_D - D :])


def standardise(hidden):
    wide = hidden[...].astype(F32)
    centred = wide - jnp.mean(wide, axis=-1, keepdims=True)
    inv_dev = lax.rsqrt(jnp.mean(centred * centred, axis=-1, keepdims=True) + EPSILON)
    return centred * inv_dev, inv_dev


def time_forward(hidden, w_qkv, w_proj, gain, qkv, probs, mix, out, acc):
    standard, _ = standardise(hidden)
    normed = (standard * gain[...]).astype(BF)
    qkv[:, :HALF_QKV] = nn(normed, w_qkv[0]).astype(BF)
    qkv[:, HALF_QKV:] = nn(normed, w_qkv[1, :, 2 * HALF_QKV - 3 * D :]).astype(BF)
    attend(qkv, probs, acc, True)
    mix[...] = acc[...].astype(BF)
    project(mix, w_proj, hidden, out)


def time_backward(hidden, cot, w_qkv, w_proj, gain, qkv, probs, grad_in, gain_term, grad, acc):
    grad[...] = back_project(cot, w_proj).astype(BF)
    attend_back(qkv, probs, grad, acc)
    low = acc[...].astype(BF)
    grad_normed = nt(low[:, :HALF_QKV], w_qkv[0]) + nt(
        low[:, HALF_QKV:], w_qkv[1, :, 2 * HALF_QKV - 3 * D :]
    )
    standard, inv_dev = standardise(hidden)
    scaled = grad_normed * gain[...]
    correction = (
        scaled
        - jnp.mean(scaled, axis=-1, keepdims=True)
        - standard * jnp.mean(scaled * standard, axis=-1, keepdims=True)
    )
    grad_in[...] = (cot[...].astype(F32) + correction * inv_dev).astype(BF)
    gain_term[...] = jnp.sum(grad_normed * standard, axis=0, keepdims=True)


def space_backward(qkv, probs, grad_in, w, out, grad, acc):
    grad[...] = back_project(grad_in, w).astype(BF)
    attend_back(qkv, probs, grad, acc)
    out[...] = acc[...].astype(BF)


def call(kernel, outs, scratch, *args):
    return pl.pallas_call(
        kernel,
        out_shape=tuple(jax.ShapeDtypeStruct(s, t) for s, t in outs),
        in_specs=[VMEM] * len(args),
        out_specs=(VMEM,) * len(outs),
        scratch_shapes=[pltpu.VMEM(s, t) for s, t in scratch],
        compiler_params=pltpu.CompilerParams(vmem_limit_bytes=50 * 2**20),
    )(*args)


def exchange(rows, axes):
    return lax.all_to_all(rows, axes, split_axis=0, concat_axis=0, tiled=True)


def gather_rows(shard, half):
    core = lax.axis_index("core")
    rows, cols = shard.shape
    piece = lax.dynamic_slice(shard, (0, core * (cols - half)), (rows, half))
    full = exchange(jnp.broadcast_to(piece[None], (8, rows, half)).reshape(8 * rows, half), FS)
    both = exchange(jnp.broadcast_to(full[None], (2, 8 * rows, half)).reshape(16 * rows, half), "core")
    return both.reshape(2, 8 * rows, half)


def swap(value):
    return lax.ppermute(value, "core", [(0, 1), (1, 0)])


def split(value, parts):
    out = []
    for _ in range(parts):
        low = value.astype(BF)
        out.append(low)
        value = value - low.astype(F32)
    return out


def add_blocks(blocks):
    return jnp.sum(blocks.astype(F32), axis=0)


def core_columns(rows, core):
    return lax.dynamic_index_in_dim(rows.reshape(TOK, 16, 2, 36), core, 2, False).reshape(TOK, 576)


def term_of_chip(left, left_other, right, core):
    mine = core_columns(right, core)
    theirs = swap(core_columns(right, 1 - core))
    return (tn(mine, left) + tn(theirs, left_other)).astype(BF)


def body(block_in, spatial_qkv, cotangent, w_sproj, w_tqkv, w_tproj, t_gain):
    core = lax.axis_index("core")
    block_rows = block_in.reshape(TOK, D)
    qkv = spatial_qkv.reshape(TOK, 3 * D)
    gain = t_gain.reshape(1, D)
    full_sproj = gather_rows(w_sproj, HALF_D)
    full_tqkv = gather_rows(w_tqkv, HALF_QKV)
    full_tproj = gather_rows(w_tproj, HALF_D)
    cot_cols = exchange(cotangent.reshape(TOK, D), SEQ)

    probs_shape = ((HEADS, TOK, TOK), BF)
    rows_shape = ((TOK, D), BF)
    wide_shape = ((TOK, 3 * D), BF)
    space_mix, space_probs = call(space_forward, (rows_shape, probs_shape), [((TOK, D), F32)], qkv)
    space_mix_other = swap(space_mix)
    (hidden,) = call(project, (rows_shape,), [], space_mix, full_sproj, block_rows)
    hidden_cols = exchange(hidden, SEQ)

    time_qkv, time_probs, time_mix, out_cols = call(
        time_forward,
        (wide_shape, probs_shape, rows_shape, rows_shape),
        [((TOK, D), F32)],
        hidden_cols, full_tqkv, full_tproj, gain,
    )
    grad_cols, gain_term = call(
        time_backward,
        (rows_shape, ((1, D), F32)),
        [((TOK, D), BF), ((TOK, 3 * D), F32)],
        hidden_cols, cot_cols, full_tqkv, full_tproj, gain, time_qkv, time_probs,
    )
    grad_in = exchange(grad_cols, SEQ)
    block_out = exchange(out_cols, SEQ)

    term_tproj = term_of_chip(time_mix, swap(time_mix), cot_cols, core)
    sum_tproj = add_blocks(exchange(term_tproj, "x").reshape(4, 144, D))

    (grad_qkv,) = call(
        space_backward,
        (wide_shape,),
        [((TOK, D), BF), ((TOK, 3 * D), F32)],
        qkv, space_probs, grad_in, full_sproj,
    )

    gain_pair = gain_term + swap(gain_term)
    gain_rows = jnp.pad(jnp.concatenate(split(gain_pair, 3)), ((0, 13), (0, 0)))
    term_sproj = term_of_chip(space_mix, space_mix_other, grad_in, core)
    sent = jnp.concatenate(
        [term_sproj.reshape(4, 144, D), jnp.broadcast_to(gain_rows, (4, 16, D))], axis=1
    )
    got = add_blocks(exchange(sent.reshape(640, D), "x").reshape(4, 160, D))
    gain_sum = jnp.sum(got[144:], axis=0, keepdims=True)

    gain_rows = jnp.broadcast_to(jnp.concatenate(split(gain_sum, 3)), (4, 3, D))
    sent = jnp.concatenate(
        [
            got[:144].astype(BF).reshape(4, 36, D),
            sum_tproj.astype(BF).reshape(4, 36, D),
            jnp.pad(gain_rows, ((0, 0), (0, 5), (0, 0))),
        ],
        axis=1,
    )
    got = add_blocks(exchange(sent.reshape(320, D), "zh").reshape(4, 80, D))
    gain_sum = jnp.sum(got[72:], axis=0, keepdims=True)

    terms = got[:72].astype(BF).reshape(72, 8, 144).transpose(1, 0, 2)
    gain_rows = jnp.broadcast_to(jnp.concatenate(split(gain_sum, 3)).reshape(24, 144), (8, 24, 144))
    sent = jnp.concatenate([terms, gain_rows], axis=1)
    got = add_blocks(exchange(sent.reshape(768, 144), FS).reshape(8, 96, 144))
    grad_sproj = got[:36].T
    grad_tproj = got[36:72].T
    grad_gain = jnp.sum(got[72:].reshape(3, D), axis=0)

    shape = block_in.shape
    return (
        block_out.reshape(shape),
        grad_in.reshape(shape),
        grad_qkv.reshape(spatial_qkv.shape),
        grad_sproj,
        grad_tproj,
        grad_gain,
    )


def solution(mesh):
    fine = Mesh(mesh.devices.reshape(4, 4, 2, 4, 2), ("x", "zh", "core", "y", "zl"))
    tokens = P(FS, SEQ, None, None)
    weights = P(FS, None)
    return jax.shard_map(
        body,
        mesh=fine,
        in_specs=(tokens, tokens, tokens, weights, weights, weights, P()),
        out_specs=(tokens, tokens, tokens, P(FS, SEQ), P(FS, SEQ), P()),
        check_vma=False,
    )
```

```python
import math

import jax
import jax.numpy as jnp
from jax import lax
from jax.experimental import pallas as pl
from jax.experimental.pallas import tpu as pltpu
from jax.sharding import Mesh, PartitionSpec as P

HEADS = 16
HD = 72
D = 1152
TOK = 256
EPSILON = 1e-06
SCALE = 1.0 / math.sqrt(HD)
LOG2E = 1.4426950408889634
HALF_D = 640
HALF_QKV = 1792
SHARD = 144
BF = jnp.bfloat16
F32 = jnp.float32
FS = ("y", "zl")
SEQ = ("x", "zh", "core")
VMEM = pl.BlockSpec(memory_space=pltpu.VMEM)
NT = (((1,), (1,)), ((), ()))
TN = (((0,), (0,)), ((), ()))


def nn(a, b):
    return jnp.dot(a, b, preferred_element_type=F32)


def nt(a, b):
    return lax.dot_general(a, b, NT, preferred_element_type=F32)


def tn(a, b):
    return lax.dot_general(a, b, TN, preferred_element_type=F32)


def window(head):
    lo = HD * head // 128 * 128
    hi = -(-(HD * head + HD) // 128) * 128
    cols = lax.broadcasted_iota(jnp.int32, (TOK, hi - lo), 1)
    inside = (cols >= HD * head - lo) & (cols < HD * head + HD - lo)
    return lo, hi, inside


def keep(inside, block):
    return jnp.where(inside, block, jnp.zeros_like(block))


def same_patch():
    rows = lax.broadcasted_iota(jnp.int32, (TOK, TOK), 0)
    cols = lax.broadcasted_iota(jnp.int32, (TOK, TOK), 1)
    return (rows & 7) == (cols & 7)


def attend(qkv, probs, acc, temporal):
    acc[...] = jnp.zeros_like(acc)
    for head in range(HEADS):
        lo, hi, inside = window(head)
        q = qkv[:, lo:hi]
        k = keep(inside, qkv[:, D + lo : D + hi])
        v = keep(inside, qkv[:, 2 * D + lo : 2 * D + hi])
        s = nt(q, k) * (SCALE * LOG2E)
        if temporal:
            s = jnp.where(same_patch(), s, -jnp.inf)
        e = jnp.exp2(s - jnp.max(s, axis=-1, keepdims=True))
        p = (e * (1.0 / jnp.sum(e, axis=-1, keepdims=True))).astype(BF)
        probs[head] = p
        acc[:, lo:hi] += nn(p, v)


def attend_back(qkv, probs, grad, acc):
    acc[...] = jnp.zeros_like(acc)
    for head in range(HEADS):
        lo, hi, inside = window(head)
        q = keep(inside, qkv[:, lo:hi])
        k = keep(inside, qkv[:, D + lo : D + hi])
        v = qkv[:, 2 * D + lo : 2 * D + hi]
        g = keep(inside, grad[:, lo:hi])
        p_low = probs[head]
        p = p_low.astype(F32)
        dp = nt(g, v)
        t = p * dp
        ds = ((t - p * jnp.sum(t, axis=-1, keepdims=True)) * SCALE).astype(BF)
        acc[:, lo:hi] += nn(ds, k)
        acc[:, D + lo : D + hi] += tn(ds, q)
        acc[:, 2 * D + lo : 2 * D + hi] += tn(p_low, g)


def space_forward(qkv, mix, probs, acc):
    attend(qkv, probs, acc, False)
    mix[...] = acc[...].astype(BF)


def project(mix, w, residual, out):
    out[:, :HALF_D] = (residual[:, :HALF_D].astype(F32) + nn(mix[...], w[0])).astype(BF)
    out[:, HALF_D:] = (
        residual[:, HALF_D:].astype(F32) + nn(mix[...], w[1, :, 2 * HALF_D - D :])
    ).astype(BF)


def back_project(grad, w):
    return nt(grad[:, :HALF_D], w[0]) + nt(grad[:, HALF_D:], w[1, :, 2 * HALF_D - D :])


def standardise(hidden):
    wide = hidden[...].astype(F32)
    centred = wide - jnp.mean(wide, axis=-1, keepdims=True)
    inv_dev = lax.rsqrt(jnp.mean(centred * centred, axis=-1, keepdims=True) + EPSILON)
    return centred * inv_dev, inv_dev


def load(ids, own, mine, theirs, full, sem):
    place, core = ids[0], ids[1]
    copies = []
    for half in range(2):
        copies.append((own.at[half], full.at[half, pl.ds(pl.multiple_of(place * SHARD, 16), SHARD)]))
    for step in range(1, 8):
        rows = pl.ds(pl.multiple_of(((place + 8 - step) & 7) * SHARD, 16), SHARD)
        part = pl.ds((step - 1) * SHARD, SHARD)
        copies.append((mine.at[part], full.at[core, rows]))
        copies.append((theirs.at[part], full.at[1 - core, rows]))
    copies = [pltpu.make_async_copy(src, dst, sem) for src, dst in copies]
    for copy in copies:
        copy.start()
    return copies


def finish(copies):
    for copy in copies:
        copy.wait()


def project_first(ids, own, mine, theirs, mix, residual, out, full, sem):
    finish(load(ids, own, mine, theirs, full, sem))
    project(mix, full, residual, out)


def time_forward(ids, own, mine, theirs, hidden, gain, qkv, probs, mix, out, full, acc, sem):
    copies = load(ids, own, mine, theirs, full, sem)
    standard, _ = standardise(hidden)
    normed = (standard * gain[...]).astype(BF)
    finish(copies)
    qkv[:, :HALF_QKV] = nn(normed, full[0, :, :HALF_QKV]).astype(BF)
    qkv[:, HALF_QKV:] = nn(normed, full[1, :, 2 * HALF_QKV - 3 * D : HALF_QKV]).astype(BF)
    attend(qkv, probs, acc, True)
    mix[...] = acc[...].astype(BF)
    project(mix, full.at[:, :, HALF_QKV:], hidden, out)


def time_backward(
    ids, own, mine, theirs, hidden, cot, gain, qkv, probs, block, sent, gain_term, full, grad, acc, sem
):
    finish(load(ids, own, mine, theirs, full, sem))
    grad[...] = back_project(cot, full.at[:, :, HALF_QKV:]).astype(BF)
    attend_back(qkv, probs, grad, acc)
    low = acc[...].astype(BF)
    grad_normed = nt(low[:, :HALF_QKV], full[0, :, :HALF_QKV]) + nt(
        low[:, HALF_QKV:], full[1, :, 2 * HALF_QKV - 3 * D : HALF_QKV]
    )
    standard, inv_dev = standardise(hidden)
    scaled = grad_normed * gain[...]
    correction = (
        scaled
        - jnp.mean(scaled, axis=-1, keepdims=True)
        - standard * jnp.mean(scaled * standard, axis=-1, keepdims=True)
    )
    grad_in = cot[...].astype(F32) + correction * inv_dev
    both = jnp.concatenate(
        [grad_in.reshape(32, 8, D), block[...].astype(F32).reshape(32, 8, D)], axis=1
    )
    sent[...] = both.astype(BF)
    gain_sum = jnp.sum(grad_normed * standard, axis=0, keepdims=True)
    for part in range(4):
        gain_term[part : part + 1, :] = gain_sum[:, 288 * part : 288 * part + 288]


def space_backward(ids, own, mine, theirs, qkv, probs, grad_in, out, full, grad, acc, sem):
    finish(load(ids, own, mine, theirs, full, sem))
    grad[...] = back_project(grad_in, full).astype(BF)
    attend_back(qkv, probs, grad, acc)
    out[...] = acc[...].astype(BF)


def pick(ids, rows, mine, theirs):
    row = lax.broadcasted_iota(jnp.int32, (D, D // 2), 0)
    col = lax.broadcasted_iota(jnp.int32, (D, D // 2), 1)
    group = lax.shift_right_logical(col * 1821, 16)
    for out, core in ((mine, ids[1]), (theirs, 1 - ids[1])):
        chosen = row == col + 36 * (group + core)
        out[...] = nn(rows[...], jnp.where(chosen, 1.0, 0.0).astype(BF)).astype(BF)


def chip_term(left, left_other, right, right_other, gain, out):
    term = tn(right[...], left[...]) + tn(right_other[...], left_other[...])
    high = gain[...].astype(BF).astype(F32)
    extra = jnp.concatenate([high, gain[...] - high, jnp.zeros((8, 288), F32)], axis=0).astype(BF)
    for x in range(4):
        for y in range(4):
            piece = term[144 * x : 144 * x + 144, 288 * y : 288 * y + 288]
            out[4 * x + y, :144] = piece.astype(BF)
            out[4 * x + y, 144:] = extra


def fold(first, second, out):
    total = [jnp.sum(ref[...].astype(F32), axis=0) for ref in (first, second)]
    gain = total[0][144:148] + total[0][148:152]
    high = gain.astype(BF).astype(F32)
    extra = jnp.concatenate([high, gain - high, jnp.zeros((4, 288), F32)], axis=0)
    for zh in range(4):
        rows = [t[36 * zh : 36 * zh + 36] for t in total]
        for zl in range(2):
            cols = [r[:, 144 * zl : 144 * zl + 144] for r in rows]
            piece = jnp.concatenate([jnp.concatenate(cols, axis=1), extra], axis=0)
            out[2 * zh + zl] = piece.astype(BF)


def call(kernel, outs, scratch, *args, smem=0, hbm=0):
    specs = [pl.BlockSpec(memory_space=pltpu.SMEM)] * smem
    specs += [pl.BlockSpec(memory_space=pl.ANY)] * hbm
    specs += [VMEM] * (len(args) - smem - hbm)
    return pl.pallas_call(
        kernel,
        out_shape=tuple(jax.ShapeDtypeStruct(s, t) for s, t in outs),
        in_specs=specs,
        out_specs=(VMEM,) * len(outs),
        scratch_shapes=scratch,
        compiler_params=pltpu.CompilerParams(vmem_limit_bytes=44 * 2**20),
    )(*args)


def exchange(rows, axes):
    return lax.all_to_all(rows, axes, split_axis=0, concat_axis=0, tiled=True)


def swap(value):
    return lax.ppermute(value, "core", [(0, 1), (1, 0)])


def halves(shard, half):
    return jnp.stack([shard[:, :half], shard[:, shard.shape[1] - half :]])


def gather_rows(own, core):
    piece = lax.dynamic_index_in_dim(own, core, 0, False)
    got = [
        lax.ppermute(piece, FS, [(i, (i + step) % 8) for i in range(8)]) for step in range(1, 8)
    ]
    return jnp.concatenate(got, axis=0)


def body(block_in, spatial_qkv, cotangent, w_sproj, w_tqkv, w_tproj, t_gain):
    core = lax.axis_index("core")
    ids = jnp.stack([lax.axis_index(FS), core]).astype(jnp.int32)
    block_rows = block_in.reshape(TOK, D)
    qkv = spatial_qkv.reshape(TOK, 3 * D)
    gain = t_gain.reshape(1, D)
    own_space = halves(w_sproj, HALF_D)
    own_time = jnp.concatenate([halves(w_tqkv, HALF_QKV), halves(w_tproj, HALF_D)], axis=2)
    own_time, mine_space = lax.optimization_barrier((own_time, gather_rows(own_space, core)))
    space_weights = (own_space, mine_space, swap(mine_space))
    mine_time = gather_rows(own_time, core)
    time_weights = (own_time, mine_time, swap(mine_time))
    cot_cols = exchange(cotangent.reshape(TOK, D), SEQ)

    rows_shape = ((TOK, D), BF)
    half_shape = ((TOK, D // 2), BF)
    wide_shape = ((TOK, 3 * D), BF)
    probs_shape = ((HEADS, TOK, TOK), BF)
    sem = pltpu.SemaphoreType.DMA
    full_space = pltpu.VMEM((2, D, HALF_D), BF)
    full_time = pltpu.VMEM((2, D, HALF_QKV + HALF_D), BF)
    rows_acc = pltpu.VMEM((TOK, D), F32)
    wide_acc = pltpu.VMEM((TOK, 3 * D), F32)
    rows_low = pltpu.VMEM((TOK, D), BF)

    space_mix, space_probs = call(space_forward, (rows_shape, probs_shape), [rows_acc], qkv)
    space_mix_other = swap(space_mix)
    (hidden,) = call(
        project_first, (rows_shape,), [full_space, sem], ids, *space_weights, space_mix, block_rows, smem=1, hbm=3
    )
    hidden_cols = exchange(hidden, SEQ)

    time_qkv, time_probs, time_mix, out_cols = call(
        time_forward,
        (wide_shape, probs_shape, rows_shape, rows_shape),
        [full_time, rows_acc, sem],
        ids, *time_weights, hidden_cols, gain,
        smem=1, hbm=3,
    )
    cot_mine, cot_theirs = call(pick, (half_shape, half_shape), [], ids, cot_cols, smem=1)
    term_shape = ((16, 160, 288), BF)
    (term_tproj,) = call(
        chip_term, (term_shape,), [],
        time_mix, swap(time_mix), cot_mine, swap(cot_theirs), jnp.zeros((4, 288), F32),
    )
    hidden_cols, term_tproj = lax.optimization_barrier((hidden_cols, term_tproj))
    sum_tproj = exchange(term_tproj, ("x", "y"))

    sent, gain_term = call(
        time_backward,
        (((32, 16, D), BF), ((4, 288), F32)),
        [full_time, rows_low, wide_acc, sem],
        ids, *time_weights, hidden_cols, cot_cols, gain, time_qkv, time_probs, out_cols,
        smem=1, hbm=3,
    )
    got = exchange(sent, SEQ)
    grad_in = got[:, :8].reshape(TOK, D)
    block_out = got[:, 8:]

    in_mine, in_theirs = call(pick, (half_shape, half_shape), [], ids, grad_in, smem=1)
    gain_pair = gain_term + swap(gain_term)
    (term_sproj,) = call(
        chip_term, (term_shape,), [], space_mix, space_mix_other, in_mine, swap(in_theirs), gain_pair
    )
    grad_in_later, term_sproj = lax.optimization_barrier((grad_in, term_sproj))
    sum_sproj = exchange(term_sproj, ("x", "y"))
    (grad_qkv,) = call(
        space_backward,
        (wide_shape,),
        [full_space, rows_low, wide_acc, sem],
        ids, *space_weights, qkv, space_probs, grad_in_later,
        smem=1, hbm=3,
    )
    (pieces,) = call(fold, (((8, 48, 288), BF),), [], sum_sproj, sum_tproj)
    last = jnp.sum(exchange(pieces, ("zh", "zl")).astype(F32), axis=0)

    shape = block_in.shape
    return (
        block_out.reshape(shape),
        grad_in.reshape(shape),
        grad_qkv.reshape(spatial_qkv.shape),
        last[:36, :144].T,
        last[:36, 144:].T,
        (last[36:40] + last[40:44]).reshape(D),
    )


def solution(mesh):
    fine = Mesh(mesh.devices.reshape(4, 4, 2, 4, 2), ("x", "zh", "core", "y", "zl"))
    tokens = P(FS, SEQ, None, None)
    weights = P(FS, None)
    return jax.shard_map(
        body,
        mesh=fine,
        in_specs=(tokens, tokens, tokens, weights, weights, weights, P()),
        out_specs=(tokens, tokens, tokens, P(FS, SEQ), P(FS, SEQ), P()),
        check_vma=False,
    )
```

```python
import math

import jax
import jax.numpy as jnp
from jax import lax
from jax.experimental import pallas as pl
from jax.experimental.pallas import tpu as pltpu
from jax.sharding import Mesh, PartitionSpec as P

HEADS = 16
HD = 72
D = 1152
TOK = 256
EPSILON = 1e-06
SCALE = 1.0 / math.sqrt(HD)
LOG2E = 1.4426950408889634
HALF_D = 640
HALF_QKV = 1792
SHARD = 144
QUARTER = 256
REST = 1408
BF = jnp.bfloat16
F32 = jnp.float32
FS = ("y", "zl")
SEQ = ("x", "zh", "core")
VMEM = pl.BlockSpec(memory_space=pltpu.VMEM)
NT = (((1,), (1,)), ((), ()))
TN = (((0,), (0,)), ((), ()))


def nn(a, b):
    return jnp.dot(a, b, preferred_element_type=F32)


def nt(a, b):
    return lax.dot_general(a, b, NT, preferred_element_type=F32)


def tn(a, b):
    return lax.dot_general(a, b, TN, preferred_element_type=F32)


def window(head):
    lo = HD * head // 128 * 128
    hi = -(-(HD * head + HD) // 128) * 128
    cols = lax.broadcasted_iota(jnp.int32, (TOK, hi - lo), 1)
    inside = (cols >= HD * head - lo) & (cols < HD * head + HD - lo)
    return lo, hi, inside


def keep(inside, block):
    return jnp.where(inside, block, jnp.zeros_like(block))


def same_patch():
    rows = lax.broadcasted_iota(jnp.int32, (TOK, TOK), 0)
    cols = lax.broadcasted_iota(jnp.int32, (TOK, TOK), 1)
    return (rows & 7) == (cols & 7)


def attend(qkv, probs, acc, temporal):
    acc[...] = jnp.zeros_like(acc)
    for head in range(HEADS):
        lo, hi, inside = window(head)
        q = qkv[:, lo:hi]
        k = keep(inside, qkv[:, D + lo : D + hi])
        v = keep(inside, qkv[:, 2 * D + lo : 2 * D + hi])
        s = nt(q, k) * (SCALE * LOG2E)
        if temporal:
            s = jnp.where(same_patch(), s, -jnp.inf)
        e = jnp.exp2(s - jnp.max(s, axis=-1, keepdims=True))
        p = (e * (1.0 / jnp.sum(e, axis=-1, keepdims=True))).astype(BF)
        probs[head] = p
        acc[:, lo:hi] += nn(p, v)


def attend_back(qkv, probs, grad, acc):
    acc[...] = jnp.zeros_like(acc)
    for head in range(HEADS):
        lo, hi, inside = window(head)
        q = keep(inside, qkv[:, lo:hi])
        k = keep(inside, qkv[:, D + lo : D + hi])
        v = qkv[:, 2 * D + lo : 2 * D + hi]
        g = keep(inside, grad[:, lo:hi])
        p_low = probs[head]
        p = p_low.astype(F32)
        dp = nt(g, v)
        t = p * dp
        ds = ((t - p * jnp.sum(t, axis=-1, keepdims=True)) * SCALE).astype(BF)
        acc[:, lo:hi] += nn(ds, k)
        acc[:, D + lo : D + hi] += tn(ds, q)
        acc[:, 2 * D + lo : 2 * D + hi] += tn(p_low, g)


def space_forward(qkv, mix, probs, acc):
    attend(qkv, probs, acc, False)
    mix[...] = acc[...].astype(BF)


def project(mix, w, residual, out):
    out[:, :HALF_D] = (residual[:, :HALF_D].astype(F32) + nn(mix[...], w[0])).astype(BF)
    out[:, HALF_D:] = (
        residual[:, HALF_D:].astype(F32) + nn(mix[...], w[1, :, 2 * HALF_D - D :])
    ).astype(BF)


def back_project(grad, w):
    return nt(grad[:, :HALF_D], w[0]) + nt(grad[:, HALF_D:], w[1, :, 2 * HALF_D - D :])


def standardise(hidden):
    wide = hidden[...].astype(F32)
    centred = wide - jnp.mean(wide, axis=-1, keepdims=True)
    inv_dev = lax.rsqrt(jnp.mean(centred * centred, axis=-1, keepdims=True) + EPSILON)
    return centred * inv_dev, inv_dev


def load(ids, parts, full, sem):
    y, core, x, zl = ids[0], ids[1], ids[2], ids[3]
    copies = []
    for index, (mine, theirs, start, width, place) in enumerate(parts):
        if place <= 0 and index:
            place = pl.multiple_of(((x + 4 + place) & 3) * QUARTER, 128)
        for half, source in ((core, mine), (1 - core, theirs)):
            for step in range(8):
                shard = 2 * ((y + 4 - step // 2) & 3) + ((zl + step) & 1)
                rows = pl.ds(pl.multiple_of(shard * SHARD, 16), SHARD)
                copies.append(
                    pltpu.make_async_copy(
                        source.at[pl.ds(step * SHARD, SHARD), pl.ds(start, width)],
                        full.at[half, rows, pl.ds(place, width)],
                        sem.at[min(index, 1)],
                    )
                )
    for copy in copies:
        copy.start()
    return copies[:16], copies[16:]


def load_space(ids, mine, theirs, full, sem):
    finish(load(ids, [(mine, theirs, 0, HALF_D, 0)], full, sem)[0])


def load_time(ids, refs, full, sem):
    parts = [(refs[2], refs[3], 0, REST, 4 * QUARTER), (refs[0], refs[1], HALF_D, QUARTER, 0)]
    parts += [(refs[3 + step], refs[6 + step], 0, QUARTER, -step) for step in range(1, 4)]
    return load(ids, parts, full, sem)


def finish(copies):
    for copy in copies:
        copy.wait()


def interleave(first, second):
    parts = [part.astype(F32).reshape(32, 8, D) for part in (first, second)]
    return jnp.concatenate(parts, axis=1).astype(BF)


def project_first(ids, mine, theirs, mix, residual, cot, out, full, rows, sem):
    load_space(ids, mine, theirs, full, sem)
    project(mix, full, residual, rows)
    out[...] = interleave(rows[...], cot[...])


def time_forward(ids, *refs):
    both, gain, hidden, cot, qkv, probs, mix, out, full, acc, sem = refs[10:]
    first, second = load_time(ids, refs, full, sem)
    wide = both[...].astype(F32)
    hidden[...] = wide[:, :8].reshape(TOK, D).astype(BF)
    cot[...] = wide[:, 8:].reshape(TOK, D).astype(BF)
    standard, _ = standardise(hidden)
    normed = (standard * gain[...]).astype(BF)
    finish(first + second)
    qkv[:, :HALF_QKV] = nn(normed, full[0, :, :HALF_QKV]).astype(BF)
    qkv[:, HALF_QKV:] = nn(normed, full[1, :, 2 * HALF_QKV - 3 * D : HALF_QKV]).astype(BF)
    attend(qkv, probs, acc, True)
    mix[...] = acc[...].astype(BF)
    project(mix, full.at[:, :, HALF_QKV:], hidden, out)


def time_backward(ids, *refs):
    hidden, cot, gain, qkv, probs, block, sent, gain_term, full, grad, acc, sem = refs[10:]
    first, second = load_time(ids, refs, full, sem)
    finish(first)
    grad[...] = back_project(cot, full.at[:, :, HALF_QKV:]).astype(BF)
    attend_back(qkv, probs, grad, acc)
    finish(second)
    low = acc[...].astype(BF)
    grad_normed = nt(low[:, :HALF_QKV], full[0, :, :HALF_QKV]) + nt(
        low[:, HALF_QKV:], full[1, :, 2 * HALF_QKV - 3 * D : HALF_QKV]
    )
    standard, inv_dev = standardise(hidden)
    scaled = grad_normed * gain[...]
    correction = (
        scaled
        - jnp.mean(scaled, axis=-1, keepdims=True)
        - standard * jnp.mean(scaled * standard, axis=-1, keepdims=True)
    )
    grad_in = cot[...].astype(F32) + correction * inv_dev
    sent[...] = interleave(grad_in, block[...])
    gain_sum = jnp.sum(grad_normed * standard, axis=0, keepdims=True)
    for part in range(4):
        gain_term[part : part + 1, :] = gain_sum[:, 288 * part : 288 * part + 288]


def space_backward(ids, mine, theirs, qkv, probs, grad_in, out, full, grad, acc, sem):
    load_space(ids, mine, theirs, full, sem)
    grad[...] = back_project(grad_in, full).astype(BF)
    attend_back(qkv, probs, grad, acc)
    out[...] = acc[...].astype(BF)


def transposed_term(ids, left, left_other, right, right_other):
    row = lax.broadcasted_iota(jnp.int32, (D, D // 2), 0)
    col = lax.broadcasted_iota(jnp.int32, (D, D // 2), 1)
    group = lax.shift_right_logical(col * 1821, 16)
    chosen = jnp.where(row == col + 36 * (group + ids[1]), 1.0, 0.0).astype(BF)
    mine = nn(right[...], chosen).astype(BF)
    other = nn(right_other[...], chosen).astype(BF)
    return tn(mine, left[...]) + tn(other, left_other[...])


def side_by_side(block):
    groups = [block[48 * g : 48 * g + 48] for g in range(3)]
    return jnp.concatenate(groups + [jnp.zeros((48, 32), F32)], axis=1)


def space_term(ids, left, left_other, right, right_other, gain, out):
    term = transposed_term(ids, left, left_other, right, right_other)
    high = gain[...].astype(BF).astype(F32)
    extra = jnp.concatenate([high, gain[...] - high, jnp.zeros((4, 320), F32)], axis=1)
    extra = jnp.concatenate([extra, jnp.zeros((4, 896), F32)], axis=0)
    for x in range(4):
        for y in range(4):
            piece = side_by_side(term[144 * x : 144 * x + 144, 288 * y : 288 * y + 288])
            out[4 * x + y] = jnp.concatenate([piece, extra], axis=0).astype(BF)


def time_term(ids, left, left_other, right, right_other, *refs):
    term = refs[4]
    term[...] = transposed_term(ids, left, left_other, right, right_other)
    for step in range(4):
        rows = pl.ds(pl.multiple_of(((ids[2] + step) & 3) * 144, 16), 144)
        refs[step][...] = term[rows].astype(BF)


def time_sum(ids, *refs):
    total = sum(ref[...].astype(F32) for ref in refs[:4])
    cut = refs[8]
    for y in range(4):
        cut[y] = side_by_side(total[:, 288 * y : 288 * y + 288])
    for step in range(4):
        refs[4 + step][...] = cut[(ids[0] + step) & 3].astype(BF)


def fold(first, *refs):
    out = refs[4]
    total = [jnp.sum(first[...].astype(F32), axis=0), sum(ref[...].astype(F32) for ref in refs[:4])]
    gain = total[0][48:52, :288] + total[0][48:52, 288:576]
    total = [jnp.concatenate([t[:48, 288 * g : 288 * g + 288] for g in range(3)], axis=0) for t in total]
    high = gain.astype(BF).astype(F32)
    extra = jnp.concatenate([high, gain - high, jnp.zeros((4, 288), F32)], axis=0)
    for zh in range(4):
        rows = [t[36 * zh : 36 * zh + 36] for t in total]
        for zl in range(2):
            cols = [r[:, 144 * zl : 144 * zl + 144] for r in rows]
            piece = jnp.concatenate([jnp.concatenate(cols, axis=1), extra], axis=0)
            out[2 * zh + zl] = piece.astype(BF)


def call(kernel, outs, scratch, *args, us, mib, smem=0, hbm=0):
    specs = [pl.BlockSpec(memory_space=pltpu.SMEM)] * smem
    specs += [pl.BlockSpec(memory_space=pl.ANY)] * hbm
    specs += [VMEM] * (len(args) - smem - hbm)
    return pl.pallas_call(
        kernel,
        out_shape=tuple(jax.ShapeDtypeStruct(s, t) for s, t in outs),
        in_specs=specs,
        out_specs=(VMEM,) * len(outs),
        scratch_shapes=scratch,
        cost_estimate=pl.CostEstimate(
            flops=us * 10**9, bytes_accessed=us * 3 * 10**6, transcendentals=0
        ),
        compiler_params=pltpu.CompilerParams(vmem_limit_bytes=mib * 2**20),
    )(*args)


def exchange(rows, axes):
    return lax.all_to_all(rows, axes, split_axis=0, concat_axis=0, tiled=True)


def swap(value):
    return lax.ppermute(value, "core", [(0, 1), (1, 0)])


def half_of(shard, half, core):
    return lax.dynamic_slice(shard, (0, core * (shard.shape[1] - half)), (SHARD, half))


def pair_up(piece):
    return jnp.concatenate([piece, lax.ppermute(piece, "zl", [(0, 1), (1, 0)])])


def around(value, axis):
    return [lax.ppermute(value, axis, [(i, (i + step) % 4) for i in range(4)]) for step in range(1, 4)]


def body(block_in, spatial_qkv, cotangent, w_sproj, w_tqkv, w_tproj, t_gain):
    core, x, y, zl = (lax.axis_index(name) for name in ("core", "x", "y", "zl"))
    ids = jnp.stack([y, core, x, zl]).astype(jnp.int32)
    block_rows = block_in.reshape(TOK, D)
    qkv = spatial_qkv.reshape(TOK, 3 * D)
    gain = t_gain.reshape(1, D)
    rows_shape = ((TOK, D), BF)
    wide_shape = ((TOK, 3 * D), BF)
    both_shape = ((32, 16, D), BF)
    probs_shape = ((HEADS, TOK, TOK), BF)
    sem = pltpu.SemaphoreType.DMA((2,))
    full_space = pltpu.VMEM((2, D, HALF_D), BF)
    full_time = pltpu.VMEM((2, D, HALF_QKV + HALF_D), BF)
    rows_acc = pltpu.VMEM((TOK, D), F32)
    wide_acc = pltpu.VMEM((TOK, 3 * D), F32)
    rows_low = pltpu.VMEM((TOK, D), BF)

    half_qkv = half_of(w_tqkv, HALF_QKV, core)
    quarter = lax.dynamic_slice(half_qkv, (0, QUARTER * x), (SHARD, QUARTER))
    first = jnp.concatenate([half_of(w_sproj, HALF_D, core), quarter], axis=1)
    rest = jnp.concatenate([half_qkv[:, 4 * QUARTER :], half_of(w_tproj, HALF_D, core)], axis=1)
    space_mix, space_probs = call(
        space_forward, (rows_shape, probs_shape), [rows_acc], qkv, us=40, mib=20
    )
    first_pair, rest, space_mix = lax.optimization_barrier((pair_up(first), rest, space_mix))
    space_mix_other = swap(space_mix)
    rest_pair, *first_around = lax.optimization_barrier((pair_up(rest), *around(first_pair, "y")))
    first_mine = jnp.concatenate([first_pair, *first_around])
    first_theirs = swap(first_mine)
    rest_around = around(rest_pair, "y")
    quarters = around(first_mine[:, HALF_D:], "x")
    (sent,) = call(
        project_first,
        (both_shape,),
        [full_space, rows_low, sem],
        ids, first_mine, first_theirs, space_mix, block_rows, cotangent.reshape(TOK, D),
        us=60, mib=20, smem=1, hbm=2,
    )
    got, *arrived = lax.optimization_barrier((exchange(sent, SEQ), *rest_around, *quarters))
    rest_mine, quarters = jnp.concatenate([rest_pair, *arrived[:3]]), arrived[3:]
    time_weights = (
        first_mine, first_theirs, rest_mine, swap(rest_mine), *quarters, *[swap(part) for part in quarters]
    )

    hidden_cols, cot_cols, time_qkv, time_probs, time_mix, out_cols = call(
        time_forward,
        (rows_shape, rows_shape, wide_shape, probs_shape, rows_shape, rows_shape),
        [full_time, rows_acc, sem],
        ids, *time_weights, got, gain,
        us=11, mib=60, smem=1, hbm=10,
    )
    sent, gain_term = call(
        time_backward,
        (both_shape, ((4, 288), F32)),
        [full_time, rows_low, wide_acc, sem],
        ids, *time_weights, hidden_cols, cot_cols, gain, time_qkv, time_probs, out_cols,
        us=15, mib=60, smem=1, hbm=10,
    )
    time_mix, cot_cols, sent = lax.optimization_barrier((time_mix, cot_cols, sent))
    terms = call(
        time_term,
        (((144, D), BF),) * 4,
        [pltpu.VMEM((D // 2, D), F32)],
        ids, time_mix, swap(time_mix), cot_cols, swap(cot_cols),
        us=40, mib=24, smem=1,
    )
    sums = [lax.ppermute(terms[s], "x", [(i, (i + s) % 4) for i in range(4)]) for s in range(1, 4)]
    got, *sums = lax.optimization_barrier((exchange(sent, SEQ), terms[0], *sums))
    grad_in = got[:, :8].reshape(TOK, D)
    block_out = got[:, 8:]

    gain_pair = gain_term + swap(gain_term)
    (sent,) = call(
        space_term,
        (((16, 56, 896), BF),),
        [],
        ids, space_mix, space_mix_other, grad_in, swap(grad_in), gain_pair,
        us=4, mib=24, smem=1,
    )
    grad_in_later, sent, *sums = lax.optimization_barrier((grad_in, sent, *sums))
    sum_sproj = exchange(sent, ("x", "y"))
    (grad_qkv,) = call(
        space_backward,
        (wide_shape,),
        [full_space, rows_low, wide_acc, sem],
        ids, first_mine, first_theirs, qkv, space_probs, grad_in_later,
        us=60, mib=28, smem=1, hbm=2,
    )
    cuts = call(
        time_sum, (((48, 896), BF),) * 4, [pltpu.VMEM((4, 48, 896), F32)], ids, *sums, us=2, mib=12, smem=1
    )
    sums = [lax.ppermute(cuts[s], "y", [(i, (i + s) % 4) for i in range(4)]) for s in range(1, 4)]
    grad_qkv, sum_sproj, *sums = lax.optimization_barrier((grad_qkv, sum_sproj, cuts[0], *sums))
    (pieces,) = call(fold, (((8, 48, 288), BF),), [], sum_sproj, *sums, us=2, mib=12)
    last = jnp.sum(exchange(pieces, ("zh", "zl")).astype(F32), axis=0)

    shape = block_in.shape
    return (
        block_out.reshape(shape),
        grad_in.reshape(shape),
        grad_qkv.reshape(spatial_qkv.shape),
        last[:36, :144].T,
        last[:36, 144:].T,
        (last[36:40] + last[40:44]).reshape(D),
    )


def solution(mesh):
    fine = Mesh(mesh.devices.reshape(4, 4, 2, 4, 2), ("x", "zh", "core", "y", "zl"))
    tokens = P(FS, SEQ, None, None)
    weights = P(FS, None)
    return jax.shard_map(
        body,
        mesh=fine,
        in_specs=(tokens, tokens, tokens, weights, weights, weights, P()),
        out_specs=(tokens, tokens, tokens, P(FS, SEQ), P(FS, SEQ), P()),
        check_vma=False,
    )
```

```python
import math

import jax
import jax.numpy as jnp
from jax import lax
from jax.experimental import pallas as pl
from jax.experimental.pallas import tpu as pltpu
from jax.sharding import Mesh, PartitionSpec as P

HEADS = 16
HD = 72
D = 1152
TOK = 256
EPSILON = 1e-06
SCALE = 1.0 / math.sqrt(HD)
LOG2E = 1.4426950408889634
HALF_D = 640
HALF_TIME = 2304
SHARD = 144
PART = 256
REST = 1792
PAIR = 288
BF = jnp.bfloat16
F32 = jnp.float32
FS = ("y", "zl")
SEQ = ("x", "zh", "core")
VMEM = pl.BlockSpec(memory_space=pltpu.VMEM)
NT = (((1,), (1,)), ((), ()))
TN = (((0,), (0,)), ((), ()))


def nn(a, b):
    return jnp.dot(a, b, preferred_element_type=F32)


def nt(a, b):
    return lax.dot_general(a, b, NT, preferred_element_type=F32)


def tn(a, b):
    return lax.dot_general(a, b, TN, preferred_element_type=F32)


def window(head):
    lo = HD * head // 128 * 128
    hi = -(-(HD * head + HD) // 128) * 128
    cols = lax.broadcasted_iota(jnp.int32, (TOK, hi - lo), 1)
    inside = (cols >= HD * head - lo) & (cols < HD * head + HD - lo)
    return lo, hi, inside


def keep(inside, block):
    return jnp.where(inside, block, jnp.zeros_like(block))


def same_patch(ids, bias):
    rows = lax.broadcasted_iota(jnp.int32, (TOK, TOK), 0)
    cols = lax.broadcasted_iota(jnp.int32, (TOK, TOK), 1)
    bias[...] = jnp.where((rows & 7) == (cols & 7), 0.0, -jnp.inf)


def attend(qkv, probs, acc, bias=None):
    acc[:, :D] = jnp.zeros((TOK, D), F32)
    for head in range(HEADS):
        lo, hi, inside = window(head)
        q = qkv[:, lo:hi]
        k = keep(inside, qkv[:, D + lo : D + hi])
        v = keep(inside, qkv[:, 2 * D + lo : 2 * D + hi])
        s = nt(q, k) * (SCALE * LOG2E)
        if bias is not None:
            s = s + bias[...]
        e = jnp.exp2(s - jnp.max(s, axis=-1, keepdims=True))
        p = (e * (1.0 / jnp.sum(e, axis=-1, keepdims=True))).astype(BF)
        probs[head] = p
        acc[:, lo:hi] += nn(p, v)


def attend_back(qkv, probs, grad, acc):
    acc[...] = jnp.zeros_like(acc)
    for head in range(HEADS):
        lo, hi, inside = window(head)
        q = keep(inside, qkv[:, lo:hi])
        k = keep(inside, qkv[:, D + lo : D + hi])
        v = qkv[:, 2 * D + lo : 2 * D + hi]
        g = keep(inside, grad[:, lo:hi])
        p_low = probs[head]
        p = p_low.astype(F32)
        dp = nt(g, v)
        t = p * dp
        ds = ((t - p * jnp.sum(t, axis=-1, keepdims=True)) * SCALE).astype(BF)
        acc[:, lo:hi] += nn(ds, k)
        acc[:, D + lo : D + hi] += tn(ds, q)
        acc[:, 2 * D + lo : 2 * D + hi] += tn(p_low, g)


def space_forward(qkv, mix, probs, acc):
    attend(qkv, probs, acc)
    mix[...] = acc[...].astype(BF)


def project(mix, w, residual, out):
    out[:, :HALF_D] = (residual[:, :HALF_D].astype(F32) + nn(mix[...], w[0])).astype(BF)
    out[:, HALF_D:] = (
        residual[:, HALF_D:].astype(F32) + nn(mix[...], w[1, :, 2 * HALF_D - D :])
    ).astype(BF)


def back_project(grad, w):
    return nt(grad[:, :HALF_D], w[0]) + nt(grad[:, HALF_D:], w[1, :, 2 * HALF_D - D :])


def standardise(hidden):
    wide = hidden[...].astype(F32)
    centred = wide - jnp.mean(wide, axis=-1, keepdims=True)
    inv_dev = lax.rsqrt(jnp.mean(centred * centred, axis=-1, keepdims=True) + EPSILON)
    return centred * inv_dev, inv_dev


def load(ids, parts, full, sem):
    y, core = ids[0], ids[1]
    copies = []
    for mine, theirs, start, width, place in parts:
        for half, sources in ((core, mine), (1 - core, theirs)):
            for step in range(4):
                rows = pl.ds(pl.multiple_of(((y + 4 - step) & 3) * PAIR, 16), PAIR)
                copies.append(
                    pltpu.make_async_copy(
                        sources[step].at[:, pl.ds(start, width)], full.at[half, rows, pl.ds(place, width)], sem
                    )
                )
    for copy in copies:
        copy.start()
    return copies


def pairs(ref, first=0):
    return [ref.at[pl.ds(PAIR * (first + step), PAIR)] for step in range(4)]


def load_space(ids, refs, full, sem):
    finish(load(ids, [(pairs(refs[0]), pairs(refs[1]), 0, HALF_D, 0)], full, sem))


def load_time(ids, refs, full, sem):
    def place(step):
        return pl.multiple_of(((ids[2] + step) & 1) * PART, 128)

    parts = [(refs[:4], refs[4:8], 0, REST, 2 * PART)]
    parts += [(pairs(refs[8 + s]), pairs(refs[10], 4 * s), 0, PART, place(s)) for s in range(2)]
    return load(ids, parts, full, sem)


def finish(copies):
    for copy in copies:
        copy.wait()


def interleave(first, second):
    parts = [part.astype(F32).reshape(32, 8, D) for part in (first, second)]
    return jnp.concatenate(parts, axis=1).astype(BF)


def project_first(ids, *refs):
    mix, residual, cot, out, full, rows, sem = refs[2:]
    load_space(ids, refs, full, sem)
    project(mix, full, residual, rows)
    out[...] = interleave(rows[...], cot[...])


def time_block(ids, *refs):
    both, bias, gain, mix, cot, grad_cols, sent, gain_term, full, qkv, probs, hidden, out, grad, acc, sem = refs[11:]
    copies = load_time(ids, refs, full, sem)
    wide = both[...].astype(F32)
    hidden[...] = wide[:, :8].reshape(TOK, D).astype(BF)
    cot[...] = wide[:, 8:].reshape(TOK, D).astype(BF)
    standard, _ = standardise(hidden)
    normed = (standard * gain[...]).astype(BF)
    finish(copies)

    qkv[:, :HALF_TIME] = nn(normed, full[0]).astype(BF)
    qkv[:, HALF_TIME:] = nn(normed, full[1, :, :D]).astype(BF)
    attend(qkv, probs, acc, bias)
    mix[...] = acc[:, :D].astype(BF)
    out[...] = (hidden[...].astype(F32) + nn(mix[...], full[1, :, D:])).astype(BF)

    grad[...] = nt(cot[...], full[1, :, D:]).astype(BF)
    attend_back(qkv, probs, grad, acc)
    low = acc[...].astype(BF)
    grad_normed = nt(low[:, :HALF_TIME], full[0]) + nt(low[:, HALF_TIME:], full[1, :, :D])
    standard, inv_dev = standardise(hidden)
    scaled = grad_normed * gain[...]
    correction = (
        scaled
        - jnp.mean(scaled, axis=-1, keepdims=True)
        - standard * jnp.mean(scaled * standard, axis=-1, keepdims=True)
    )
    grad_in = cot[...].astype(F32) + correction * inv_dev
    grad_cols[...] = grad_in.astype(BF)
    sent[...] = interleave(grad_in, out[...])
    gain_term[...] = jnp.sum(grad_normed * standard, axis=0, keepdims=True)


def space_backward(ids, *refs):
    qkv, probs, grad_in, out, full, grad, acc, sem = refs[2:]
    load_space(ids, refs, full, sem)
    grad[...] = back_project(grad_in, full).astype(BF)
    attend_back(qkv, probs, grad, acc)
    out[...] = acc[...].astype(BF)


def choose_columns(ids, chosen):
    row = lax.broadcasted_iota(jnp.int32, (D, D // 2), 0)
    col = lax.broadcasted_iota(jnp.int32, (D, D // 2), 1)
    group = lax.shift_right_logical(col * 1821, 16)
    chosen[...] = jnp.where(row == col + 36 * (group + ids[1]), 1.0, 0.0).astype(BF)


def transposed_term(chosen, left, left_other, right, right_other):
    mine = nn(right[...], chosen[...]).astype(BF)
    other = nn(right_other[...], chosen[...]).astype(BF)
    return tn(mine, left[...]) + tn(other, left_other[...])


def both_terms(ids, *refs):
    gain, chosen, outs, cut = refs[8], refs[9], refs[10:14], refs[14]
    for index in range(2):
        term = transposed_term(chosen, *refs[4 * index : 4 * index + 4])
        for y in range(4):
            cols = [term[144 * x : 144 * x + 144, 288 * y : 288 * y + 288] for x in range(4)]
            cut[y, 144 * index : 144 * index + 144] = jnp.concatenate(cols, axis=1)
    cut[:, 288:] = jnp.broadcast_to(gain[...], (4, 16, D))
    for step in range(4):
        outs[step][...] = cut[(ids[0] + step) & 3].astype(BF)


def add_first(*refs):
    out = refs[4]
    total = sum(ref[...].astype(F32) for ref in refs[:4])
    gain = jnp.concatenate([total[288:289, 288 * part : 288 * part + 288] for part in range(4)], axis=0)
    for x in range(4):
        for zh in range(4):
            for zl in range(2):
                lanes = slice(288 * x + 144 * zl, 288 * x + 144 * zl + 144)
                terms = [total[144 * i + 36 * zh : 144 * i + 36 * zh + 36, lanes] for i in range(2)]
                piece = jnp.concatenate([jnp.concatenate(terms, axis=1), gain], axis=0)
                groups = [piece[8 * g : 8 * g + 8] for g in range(5)]
                piece = jnp.concatenate(groups + [jnp.zeros((8, 96), F32)], axis=1)
                out[8 * x + 2 * zh + zl] = piece.astype(BF)


def add_last(got, out):
    total = jnp.sum(got[...].astype(F32), axis=0)
    out[...] = jnp.concatenate([total[:, 288 * g : 288 * g + 288] for g in range(5)], axis=0)


def call(kernel, outs, scratch, *args, us, mib, smem=0, hbm=0):
    specs = [pl.BlockSpec(memory_space=pltpu.SMEM)] * smem
    specs += [pl.BlockSpec(memory_space=pl.ANY)] * hbm
    specs += [VMEM] * (len(args) - smem - hbm)
    return pl.pallas_call(
        kernel,
        out_shape=tuple(jax.ShapeDtypeStruct(s, t) for s, t in outs),
        in_specs=specs,
        out_specs=(VMEM,) * len(outs),
        scratch_shapes=scratch,
        cost_estimate=pl.CostEstimate(
            flops=us * 10**9, bytes_accessed=us * 3 * 10**6, transcendentals=0
        ),
        compiler_params=pltpu.CompilerParams(vmem_limit_bytes=mib * 2**20),
    )(*args)


def exchange(rows, axes):
    return lax.all_to_all(rows, axes, split_axis=0, concat_axis=0, tiled=True)


def swap(value):
    return lax.ppermute(value, "core", [(0, 1), (1, 0)])


def half_of(shard, half, core):
    return lax.dynamic_slice(shard, (0, core * (shard.shape[1] - half)), (SHARD, half))


def pair_up(piece, zl):
    other = lax.ppermute(piece, "zl", [(0, 1), (1, 0)])
    return jnp.where(zl == 0, jnp.concatenate([piece, other]), jnp.concatenate([other, piece]))


def shift(value, axis, step):
    return lax.ppermute(value, axis, [(i, (i + step) % 4) for i in range(4)])


def around(value, axis):
    return [shift(value, axis, step) for step in range(1, 4)]


def deal(pieces, axis):
    return [shift(pieces[step], axis, step) for step in range(1, 4)]


def body(block_in, spatial_qkv, cotangent, w_sproj, w_tqkv, w_tproj, t_gain):
    core, x, y, zl = (lax.axis_index(name) for name in ("core", "x", "y", "zl"))
    ids = jnp.stack([y, core, x, zl]).astype(jnp.int32)
    block_rows = block_in.reshape(TOK, D)
    qkv = spatial_qkv.reshape(TOK, 3 * D)
    gain = t_gain.reshape(1, D)
    rows_shape = ((TOK, D), BF)
    wide_shape = ((TOK, 3 * D), BF)
    both_shape = ((32, 16, D), BF)
    probs_shape = ((HEADS, TOK, TOK), BF)
    sem = pltpu.SemaphoreType.DMA
    full_space = pltpu.VMEM((2, D, HALF_D), BF)
    full_time = pltpu.VMEM((2, D, HALF_TIME), BF)
    rows_acc = pltpu.VMEM((TOK, D), F32)
    wide_acc = pltpu.VMEM((TOK, 3 * D), F32)
    rows_low = pltpu.VMEM((TOK, D), BF)
    wide_low = pltpu.VMEM((TOK, 3 * D), BF)
    probs_low = pltpu.VMEM(*probs_shape)

    time_half = jnp.where(
        core == 0, w_tqkv[:, :HALF_TIME], jnp.concatenate([w_tqkv[:, HALF_TIME:], w_tproj], axis=1)
    )
    part = lax.dynamic_slice(time_half, (0, PART * (x % 2)), (SHARD, PART))
    first = jnp.concatenate([half_of(w_sproj, HALF_D, core), part], axis=1)
    rest = time_half[:, 2 * PART :]
    space_mix, space_probs = call(
        space_forward, (rows_shape, probs_shape), [rows_acc], qkv, us=40, mib=20
    )
    first_pair, rest, space_mix = lax.optimization_barrier((pair_up(first, zl), rest, space_mix))
    rest_pair, *arrived = lax.optimization_barrier((pair_up(rest, zl), first_pair, *around(first_pair, "y")))
    space_mine = jnp.concatenate([pair[:, :HALF_D] for pair in arrived])
    part_mine = jnp.concatenate([pair[:, HALF_D:] for pair in arrived])
    ids, space_mix, rest_pair, part_mine, space_mine, space_theirs = lax.optimization_barrier(
        (ids, space_mix, rest_pair, part_mine, space_mine, swap(space_mine))
    )
    (sent,) = call(
        project_first,
        (both_shape,),
        [full_space, rows_low, sem],
        ids, space_mine, space_theirs, space_mix, block_rows, cotangent.reshape(TOK, D),
        us=60, mib=60, smem=1, hbm=2,
    )
    (chosen,) = call(choose_columns, (((D, D // 2), BF),), [], ids, us=100, mib=60, smem=1)
    (bias,) = call(same_patch, (((TOK, TOK), F32),), [], ids, us=100, mib=60, smem=1)
    got, bias, chosen, space_mix, own_theirs, part_other, *rest_mine = lax.optimization_barrier(
        (
            exchange(sent, SEQ), bias, chosen, space_mix, swap(rest_pair),
            lax.ppermute(part_mine, "x", [(i, i ^ 1) for i in range(4)]), rest_pair, *around(rest_pair, "y"),
        )
    )
    time_weights = [*rest_mine, own_theirs, *[swap(pair) for pair in rest_mine[1:]]]
    time_weights += [part_mine, part_other, swap(jnp.concatenate([part_mine, part_other]))]

    time_mix, cot_cols, grad_cols, sent, gain_term = call(
        time_block,
        (rows_shape, rows_shape, rows_shape, both_shape, ((1, D), F32)),
        [full_time, wide_low, probs_low, rows_low, rows_low, rows_low, wide_acc, sem],
        ids, *time_weights, got, bias, gain,
        us=60, mib=60, smem=1, hbm=11,
    )
    mix_cols, time_mix, cot_cols, grad_cols, sent, gain_term = lax.optimization_barrier(
        (exchange(space_mix, SEQ), time_mix, cot_cols, grad_cols, sent, gain_term)
    )
    terms = call(
        both_terms,
        (((304, D), BF),) * 4,
        [pltpu.VMEM((4, 304, D), F32)],
        ids,
        mix_cols, swap(mix_cols), grad_cols, swap(grad_cols),
        time_mix, swap(time_mix), cot_cols, swap(cot_cols),
        gain_term + swap(gain_term), chosen,
        us=60, mib=40, smem=1,
    )
    (pieces,) = call(add_first, (((32, 8, 1536), BF),), [], terms[0], *deal(terms, "y"), us=3, mib=24)
    pieces, got = lax.optimization_barrier((pieces, exchange(sent, SEQ)))
    grad_in = got[:, :8].reshape(TOK, D)
    block_out = got[:, 8:]
    (grad_qkv,) = call(
        space_backward,
        (wide_shape,),
        [full_space, rows_low, wide_acc, sem],
        ids, space_mine, space_theirs, qkv, space_probs, grad_in,
        us=60, mib=60, smem=1, hbm=2,
    )
    last, grad_qkv = lax.optimization_barrier((exchange(pieces, ("x", "zh", "zl")), grad_qkv))
    (last,) = call(add_last, (((40, 288), F32),), [], last, us=1, mib=12)

    shape = block_in.shape
    return (
        block_out.reshape(shape),
        grad_in.reshape(shape),
        grad_qkv.reshape(spatial_qkv.shape),
        last[:36, :144].T,
        last[:36, 144:].T,
        last[36:].reshape(D),
    )


def solution(mesh):
    fine = Mesh(mesh.devices.reshape(4, 4, 2, 4, 2), ("x", "zh", "core", "y", "zl"))
    tokens = P(FS, SEQ, None, None)
    weights = P(FS, None)
    return jax.shard_map(
        body,
        mesh=fine,
        in_specs=(tokens, tokens, tokens, weights, weights, weights, P()),
        out_specs=(tokens, tokens, tokens, P(FS, SEQ), P(FS, SEQ), P()),
        check_vma=False,
    )
```

```python
import math

import jax
import jax.numpy as jnp
from jax import lax
from jax.experimental import pallas as pl
from jax.experimental.pallas import tpu as pltpu
from jax.sharding import Mesh, PartitionSpec as P

HEADS = 16
HD = 72
D = 1152
TOK = 256
EPSILON = 1e-06
SCALE = 1.0 / math.sqrt(HD)
LOG2E = 1.4426950408889634
HALF_D = 640
HALF_TIME = 2304
SHARD = 144
PART = 256
REST = 1792
PAIR = 288
BF = jnp.bfloat16
F32 = jnp.float32
FS = ("y", "zl")
SEQ = ("x", "zh", "core")
VMEM = pl.BlockSpec(memory_space=pltpu.VMEM)
NT = (((1,), (1,)), ((), ()))
TN = (((0,), (0,)), ((), ()))


def nn(a, b):
    return jnp.dot(a, b, preferred_element_type=F32)


def nt(a, b):
    return lax.dot_general(a, b, NT, preferred_element_type=F32)


def tn(a, b):
    return lax.dot_general(a, b, TN, preferred_element_type=F32)


def window(head):
    lo = HD * head // 128 * 128
    hi = -(-(HD * head + HD) // 128) * 128
    cols = lax.broadcasted_iota(jnp.int32, (TOK, hi - lo), 1)
    inside = (cols >= HD * head - lo) & (cols < HD * head + HD - lo)
    return lo, hi, inside


def keep(inside, block):
    return jnp.where(inside, block, jnp.zeros_like(block))


def same_patch(ids, bias):
    rows = lax.broadcasted_iota(jnp.int32, (TOK, TOK), 0)
    cols = lax.broadcasted_iota(jnp.int32, (TOK, TOK), 1)
    bias[...] = jnp.where((rows & 7) == (cols & 7), 0.0, -jnp.inf)


def attend(qkv, probs, acc, bias=None):
    acc[:, :D] = jnp.zeros((TOK, D), F32)
    for head in range(HEADS):
        lo, hi, inside = window(head)
        q = qkv[:, lo:hi]
        k = keep(inside, qkv[:, D + lo : D + hi])
        v = keep(inside, qkv[:, 2 * D + lo : 2 * D + hi])
        s = nt(q, k) * (SCALE * LOG2E)
        if bias is not None:
            s = s + bias[...]
        e = jnp.exp2(s - jnp.max(s, axis=-1, keepdims=True))
        p = (e * (1.0 / jnp.sum(e, axis=-1, keepdims=True))).astype(BF)
        probs[head] = p
        acc[:, lo:hi] += nn(p, v)


def attend_back(qkv, probs, grad, acc):
    acc[...] = jnp.zeros_like(acc)
    for head in range(HEADS):
        lo, hi, inside = window(head)
        q = keep(inside, qkv[:, lo:hi])
        k = keep(inside, qkv[:, D + lo : D + hi])
        v = qkv[:, 2 * D + lo : 2 * D + hi]
        g = keep(inside, grad[:, lo:hi])
        p_low = probs[head]
        p = p_low.astype(F32)
        dp = nt(g, v)
        t = p * dp
        ds = ((t - p * jnp.sum(t, axis=-1, keepdims=True)) * SCALE).astype(BF)
        acc[:, lo:hi] += nn(ds, k)
        acc[:, D + lo : D + hi] += tn(ds, q)
        acc[:, 2 * D + lo : 2 * D + hi] += tn(p_low, g)


def space_forward(qkv, mix, probs, acc):
    attend(qkv, probs, acc)
    mix[...] = acc[...].astype(BF)


def project(mix, w, residual, out):
    out[:, :HALF_D] = (residual[:, :HALF_D].astype(F32) + nn(mix[...], w[0])).astype(BF)
    out[:, HALF_D:] = (
        residual[:, HALF_D:].astype(F32) + nn(mix[...], w[1, :, 2 * HALF_D - D :])
    ).astype(BF)


def back_project(grad, w):
    return nt(grad[:, :HALF_D], w[0]) + nt(grad[:, HALF_D:], w[1, :, 2 * HALF_D - D :])


def standardise(hidden):
    wide = hidden[...].astype(F32)
    centred = wide - jnp.mean(wide, axis=-1, keepdims=True)
    inv_dev = lax.rsqrt(jnp.mean(centred * centred, axis=-1, keepdims=True) + EPSILON)
    return centred * inv_dev, inv_dev


def load(ids, parts, full, sem):
    y, core, zl = ids[0], ids[1], ids[3]
    copies = []
    for mine, theirs, start, width, place in parts:
        for half, sources in ((core, mine), (1 - core, theirs)):
            for step, source in enumerate(sources):
                shard = 2 * ((y + 4 - step % 4) & 3)
                if len(sources) == 8:
                    shard = shard + ((zl + step // 4) & 1)
                rows = pl.ds(pl.multiple_of(shard * SHARD, 16), source.shape[0])
                copies.append(
                    pltpu.make_async_copy(
                        source.at[:, pl.ds(start, width)], full.at[half, rows, pl.ds(place, width)], sem
                    )
                )
    for copy in copies:
        copy.start()
    return copies


def shards(ref, first=0):
    return [ref.at[pl.ds(SHARD * (first + step), SHARD)] for step in range(8)]


def load_space(ids, refs, full, sem):
    finish(load(ids, [(shards(refs[0]), shards(refs[1]), 0, HALF_D, 0)], full, sem))


def load_time(ids, refs, full, sem):
    def place(step):
        return pl.multiple_of(((ids[2] + step) & 1) * PART, 128)

    parts = [(refs[:4], refs[4:8], 0, REST, 2 * PART)]
    parts += [(shards(refs[8 + s]), shards(refs[10], 8 * s), 0, PART, place(s)) for s in range(2)]
    return load(ids, parts, full, sem)


def finish(copies):
    for copy in copies:
        copy.wait()


def interleave(first, second):
    parts = [part.astype(F32).reshape(32, 8, D) for part in (first, second)]
    return jnp.concatenate(parts, axis=1).astype(BF)


def project_first(ids, *refs):
    mix, residual, out, full, sem = refs[2:]
    load_space(ids, refs, full, sem)
    project(mix, full, residual, out)


def time_block(ids, *refs):
    hidden, cot, bias, gain, mix, grad_cols, sent, gain_term, full, qkv, probs, out, grad, acc, sem = refs[11:]
    copies = load_time(ids, refs, full, sem)
    standard, _ = standardise(hidden)
    normed = (standard * gain[...]).astype(BF)
    finish(copies)

    qkv[:, :HALF_TIME] = nn(normed, full[0]).astype(BF)
    qkv[:, HALF_TIME:] = nn(normed, full[1, :, :D]).astype(BF)
    attend(qkv, probs, acc, bias)
    mix[...] = acc[:, :D].astype(BF)
    out[...] = (hidden[...].astype(F32) + nn(mix[...], full[1, :, D:])).astype(BF)

    grad[...] = nt(cot[...], full[1, :, D:]).astype(BF)
    attend_back(qkv, probs, grad, acc)
    low = acc[...].astype(BF)
    grad_normed = nt(low[:, :HALF_TIME], full[0]) + nt(low[:, HALF_TIME:], full[1, :, :D])
    standard, inv_dev = standardise(hidden)
    scaled = grad_normed * gain[...]
    correction = (
        scaled
        - jnp.mean(scaled, axis=-1, keepdims=True)
        - standard * jnp.mean(scaled * standard, axis=-1, keepdims=True)
    )
    grad_in = cot[...].astype(F32) + correction * inv_dev
    grad_cols[...] = grad_in.astype(BF)
    sent[...] = interleave(grad_in, out[...])
    gain_term[...] = jnp.sum(grad_normed * standard, axis=0, keepdims=True)


def space_backward(ids, *refs):
    qkv, probs, grad_in, out, full, grad, acc, sem = refs[2:]
    load_space(ids, refs, full, sem)
    grad[...] = back_project(grad_in, full).astype(BF)
    attend_back(qkv, probs, grad, acc)
    out[...] = acc[...].astype(BF)


def choose_columns(ids, chosen):
    row = lax.broadcasted_iota(jnp.int32, (D, D // 2), 0)
    col = lax.broadcasted_iota(jnp.int32, (D, D // 2), 1)
    group = lax.shift_right_logical(col * 1821, 16)
    chosen[...] = jnp.where(row == col + 36 * (group + ids[1]), 1.0, 0.0).astype(BF)


def transposed_term(chosen, left, left_other, right, right_other):
    mine = nn(right[...], chosen[...]).astype(BF)
    other = nn(right_other[...], chosen[...]).astype(BF)
    return tn(mine, left[...]) + tn(other, left_other[...])


def both_terms(ids, *refs):
    gain, chosen, outs, cut = refs[8], refs[9], refs[10:14], refs[14]
    for index in range(2):
        term = transposed_term(chosen, *refs[4 * index : 4 * index + 4])
        for y in range(4):
            cols = [term[144 * x : 144 * x + 144, 288 * y : 288 * y + 288] for x in range(4)]
            cut[y, 144 * index : 144 * index + 144] = jnp.concatenate(cols, axis=1)
    cut[:, 288:] = jnp.broadcast_to(gain[...], (4, 16, D))
    for step in range(4):
        outs[step][...] = cut[(ids[0] + step) & 3].astype(BF)


def add_first(*refs):
    out = refs[4]
    total = sum(ref[...].astype(F32) for ref in refs[:4])
    gain = jnp.concatenate([total[288:289, 288 * part : 288 * part + 288] for part in range(4)], axis=0)
    for x in range(4):
        for zh in range(4):
            for zl in range(2):
                lanes = slice(288 * x + 144 * zl, 288 * x + 144 * zl + 144)
                terms = [total[144 * i + 36 * zh : 144 * i + 36 * zh + 36, lanes] for i in range(2)]
                piece = jnp.concatenate([jnp.concatenate(terms, axis=1), gain], axis=0)
                groups = [piece[8 * g : 8 * g + 8] for g in range(5)]
                piece = jnp.concatenate(groups + [jnp.zeros((8, 96), F32)], axis=1)
                out[8 * x + 2 * zh + zl] = piece.astype(BF)


def add_last(got, out):
    total = jnp.sum(got[...].astype(F32), axis=0)
    out[...] = jnp.concatenate([total[:, 288 * g : 288 * g + 288] for g in range(5)], axis=0)


def call(kernel, outs, scratch, *args, us, mib, smem=0, hbm=0):
    specs = [pl.BlockSpec(memory_space=pltpu.SMEM)] * smem
    specs += [pl.BlockSpec(memory_space=pl.ANY)] * hbm
    specs += [VMEM] * (len(args) - smem - hbm)
    return pl.pallas_call(
        kernel,
        out_shape=tuple(jax.ShapeDtypeStruct(s, t) for s, t in outs),
        in_specs=specs,
        out_specs=(VMEM,) * len(outs),
        scratch_shapes=scratch,
        cost_estimate=pl.CostEstimate(
            flops=us * 10**9, bytes_accessed=us * 3 * 10**6, transcendentals=0
        ),
        compiler_params=pltpu.CompilerParams(vmem_limit_bytes=mib * 2**20),
    )(*args)


def exchange(rows, axes):
    return lax.all_to_all(rows, axes, split_axis=0, concat_axis=0, tiled=True)


def swap(value):
    return lax.ppermute(value, "core", [(0, 1), (1, 0)])


def half_of(shard, half, core):
    return lax.dynamic_slice(shard, (0, core * (shard.shape[1] - half)), (SHARD, half))


def pair_up(piece, zl):
    other = lax.ppermute(piece, "zl", [(0, 1), (1, 0)])
    return jnp.where(zl == 0, jnp.concatenate([piece, other]), jnp.concatenate([other, piece]))


def shift(value, axis, step):
    return lax.ppermute(value, axis, [(i, (i + step) % 4) for i in range(4)])


def around(value, axis):
    return [shift(value, axis, step) for step in range(1, 4)]


def deal(pieces, axis):
    return [shift(pieces[step], axis, step) for step in range(1, 4)]


def body(block_in, spatial_qkv, cotangent, w_sproj, w_tqkv, w_tproj, t_gain):
    core, x, y, zl = (lax.axis_index(name) for name in ("core", "x", "y", "zl"))
    ids = jnp.stack([y, core, x, zl]).astype(jnp.int32)
    block_rows = block_in.reshape(TOK, D)
    qkv = spatial_qkv.reshape(TOK, 3 * D)
    gain = t_gain.reshape(1, D)
    rows_shape = ((TOK, D), BF)
    wide_shape = ((TOK, 3 * D), BF)
    both_shape = ((32, 16, D), BF)
    probs_shape = ((HEADS, TOK, TOK), BF)
    sem = pltpu.SemaphoreType.DMA
    full_space = pltpu.VMEM((2, D, HALF_D), BF)
    full_time = pltpu.VMEM((2, D, HALF_TIME), BF)
    rows_acc = pltpu.VMEM((TOK, D), F32)
    wide_acc = pltpu.VMEM((TOK, 3 * D), F32)
    rows_low = pltpu.VMEM((TOK, D), BF)
    wide_low = pltpu.VMEM((TOK, 3 * D), BF)
    probs_low = pltpu.VMEM(*probs_shape)

    time_half = jnp.where(
        core == 0, w_tqkv[:, :HALF_TIME], jnp.concatenate([w_tqkv[:, HALF_TIME:], w_tproj], axis=1)
    )
    part = lax.dynamic_slice(time_half, (0, PART * (x % 2)), (SHARD, PART))
    first = jnp.concatenate([half_of(w_sproj, HALF_D, core), part], axis=1)
    rest = time_half[:, 2 * PART :]
    space_mix, space_probs = call(
        space_forward, (rows_shape, probs_shape), [rows_acc], qkv, us=40, mib=20
    )
    other, rest, space_mix, cotangent, *own = lax.optimization_barrier(
        (lax.ppermute(first, "zl", [(0, 1), (1, 0)]), rest, space_mix, cotangent, first, *around(first, "y"))
    )
    rest_pair, *arrived = lax.optimization_barrier((pair_up(rest, zl), *own, other, *around(other, "y")))
    space_mine = jnp.concatenate([piece[:, :HALF_D] for piece in arrived])
    part_mine = jnp.concatenate([piece[:, HALF_D:] for piece in arrived])
    cot_cols, space_mix, space_mine, space_theirs = lax.optimization_barrier(
        (exchange(cotangent.reshape(TOK, D), SEQ), space_mix, space_mine, swap(space_mine))
    )
    (hidden,) = call(
        project_first,
        (rows_shape,),
        [full_space, sem],
        ids, space_mine, space_theirs, space_mix, block_rows,
        us=60, mib=60, smem=1, hbm=2,
    )
    hidden, late_ids = lax.optimization_barrier((hidden, ids))
    (chosen,) = call(choose_columns, (((D, D // 2), BF),), [], late_ids, us=100, mib=60, smem=1)
    (bias,) = call(same_patch, (((TOK, TOK), F32),), [], late_ids, us=100, mib=60, smem=1)
    hidden_cols, bias, chosen, space_mix, own_theirs, part_other, *rest_mine = lax.optimization_barrier(
        (
            exchange(hidden, SEQ), bias, chosen, space_mix, swap(rest_pair),
            lax.ppermute(part_mine, "x", [(i, i ^ 1) for i in range(4)]), rest_pair, *around(rest_pair, "y"),
        )
    )
    time_weights = [*rest_mine, own_theirs, *[swap(pair) for pair in rest_mine[1:]]]
    time_weights += [part_mine, part_other, swap(jnp.concatenate([part_mine, part_other]))]

    time_mix, grad_cols, sent, gain_term = call(
        time_block,
        (rows_shape, rows_shape, both_shape, ((1, D), F32)),
        [full_time, wide_low, probs_low, rows_low, rows_low, wide_acc, sem],
        ids, *time_weights, hidden_cols, cot_cols, bias, gain,
        us=60, mib=60, smem=1, hbm=11,
    )
    mix_cols, time_mix, cot_cols, grad_cols, sent, gain_term = lax.optimization_barrier(
        (exchange(space_mix, SEQ), time_mix, cot_cols, grad_cols, sent, gain_term)
    )
    terms = call(
        both_terms,
        (((304, D), BF),) * 4,
        [pltpu.VMEM((4, 304, D), F32)],
        ids,
        mix_cols, swap(mix_cols), grad_cols, swap(grad_cols),
        time_mix, swap(time_mix), cot_cols, swap(cot_cols),
        gain_term + swap(gain_term), chosen,
        us=60, mib=40, smem=1,
    )
    (pieces,) = call(add_first, (((32, 8, 1536), BF),), [], terms[0], *deal(terms, "y"), us=3, mib=24)
    pieces, got = lax.optimization_barrier((pieces, exchange(sent, SEQ)))
    grad_in = got[:, :8].reshape(TOK, D)
    block_out = got[:, 8:]
    (grad_qkv,) = call(
        space_backward,
        (wide_shape,),
        [full_space, rows_low, wide_acc, sem],
        ids, space_mine, space_theirs, qkv, space_probs, grad_in,
        us=60, mib=60, smem=1, hbm=2,
    )
    last, grad_qkv = lax.optimization_barrier((exchange(pieces, ("x", "zh", "zl")), grad_qkv))
    (last,) = call(add_last, (((40, 288), F32),), [], last, us=1, mib=12)

    shape = block_in.shape
    return (
        block_out.reshape(shape),
        grad_in.reshape(shape),
        grad_qkv.reshape(spatial_qkv.shape),
        last[:36, :144].T,
        last[:36, 144:].T,
        last[36:].reshape(D),
    )


def solution(mesh):
    fine = Mesh(mesh.devices.reshape(4, 4, 2, 4, 2), ("x", "zh", "core", "y", "zl"))
    tokens = P(FS, SEQ, None, None)
    weights = P(FS, None)
    return jax.shard_map(
        body,
        mesh=fine,
        in_specs=(tokens, tokens, tokens, weights, weights, weights, P()),
        out_specs=(tokens, tokens, tokens, P(FS, SEQ), P(FS, SEQ), P()),
        check_vma=False,
    )
```

```python
import math

import jax
import jax.numpy as jnp
from jax import lax
from jax.experimental import pallas as pl
from jax.experimental.pallas import tpu as pltpu
from jax.sharding import Mesh, PartitionSpec as P

HEADS = 16
HD = 72
D = 1152
TOK = 256
EPSILON = 1e-06
SCALE = 1.0 / math.sqrt(HD)
LOG2E = 1.4426950408889634
HALF_D = 640
HALF_TIME = 2304
SHARD = 144
PART = 256
REST = 1792
PAIR = 288
BF = jnp.bfloat16
F32 = jnp.float32
FS = ("y", "zl")
SEQ = ("x", "zh", "core")
VMEM = pl.BlockSpec(memory_space=pltpu.VMEM)
NT = (((1,), (1,)), ((), ()))
TN = (((0,), (0,)), ((), ()))


def nn(a, b):
    return jnp.dot(a, b, preferred_element_type=F32)


def nt(a, b):
    return lax.dot_general(a, b, NT, preferred_element_type=F32)


def tn(a, b):
    return lax.dot_general(a, b, TN, preferred_element_type=F32)


def window(head):
    lo = HD * head // 128 * 128
    hi = -(-(HD * head + HD) // 128) * 128
    cols = lax.broadcasted_iota(jnp.int32, (TOK, hi - lo), 1)
    inside = (cols >= HD * head - lo) & (cols < HD * head + HD - lo)
    return lo, hi, inside


def keep(inside, block):
    return jnp.where(inside, block, jnp.zeros_like(block))


def same_patch(ids, bias):
    rows = lax.broadcasted_iota(jnp.int32, (TOK, TOK), 0)
    cols = lax.broadcasted_iota(jnp.int32, (TOK, TOK), 1)
    bias[...] = jnp.where((rows & 7) == (cols & 7), 0.0, -jnp.inf)


def add_to(acc, base, head, value):
    lo, hi, _ = window(head)
    seen = window(head - 1)[1] if head else 0
    if seen > lo:
        acc[:, base + lo : base + seen] += value[:, : seen - lo]
    if hi > seen:
        acc[:, base + seen : base + hi] = value[:, seen - lo :]


def attend(qkv, probs, acc, bias=None):
    for head in range(HEADS):
        lo, hi, inside = window(head)
        q = qkv[:, lo:hi]
        k = keep(inside, qkv[:, D + lo : D + hi])
        v = keep(inside, qkv[:, 2 * D + lo : 2 * D + hi])
        s = nt(q, k) * (SCALE * LOG2E)
        if bias is not None:
            s = s + bias[...]
        e = jnp.exp2(s - jnp.max(s, axis=-1, keepdims=True))
        p = (e * (1.0 / jnp.sum(e, axis=-1, keepdims=True))).astype(BF)
        probs[head] = p
        add_to(acc, 0, head, nn(p, v))


def attend_back(qkv, probs, grad, acc):
    for head in range(HEADS):
        lo, hi, inside = window(head)
        q = keep(inside, qkv[:, lo:hi])
        k = keep(inside, qkv[:, D + lo : D + hi])
        v = qkv[:, 2 * D + lo : 2 * D + hi]
        g = keep(inside, grad[:, lo:hi])
        p_low = probs[head]
        p = p_low.astype(F32)
        dp = nt(g, v)
        t = p * dp
        ds = ((t - p * jnp.sum(t, axis=-1, keepdims=True)) * SCALE).astype(BF)
        add_to(acc, 0, head, nn(ds, k))
        add_to(acc, D, head, tn(ds, q))
        add_to(acc, 2 * D, head, tn(p_low, g))


def space_forward(qkv, mix, probs, acc):
    attend(qkv, probs, acc)
    mix[...] = acc[...].astype(BF)


def project(mix, w, residual, out):
    out[:, :HALF_D] = (residual[:, :HALF_D].astype(F32) + nn(mix[...], w[0])).astype(BF)
    out[:, HALF_D:] = (
        residual[:, HALF_D:].astype(F32) + nn(mix[...], w[1, :, 2 * HALF_D - D :])
    ).astype(BF)


def back_project(grad, w):
    return nt(grad[:, :HALF_D], w[0]) + nt(grad[:, HALF_D:], w[1, :, 2 * HALF_D - D :])


def standardise(hidden):
    wide = hidden[...].astype(F32)
    centred = wide - jnp.mean(wide, axis=-1, keepdims=True)
    inv_dev = lax.rsqrt(jnp.mean(centred * centred, axis=-1, keepdims=True) + EPSILON)
    return centred * inv_dev, inv_dev


def load(ids, parts, full, sem):
    y, core, zl = ids[0], ids[1], ids[3]
    copies = []
    for mine, theirs, start, width, place in parts:
        for half, sources in ((core, mine), (1 - core, theirs)):
            for step, source in enumerate(sources):
                shard = 2 * ((y + 4 - step % 4) & 3)
                if len(sources) == 8:
                    shard = shard + ((zl + step // 4) & 1)
                rows = pl.ds(pl.multiple_of(shard * SHARD, 16), source.shape[0])
                copies.append(
                    pltpu.make_async_copy(
                        source.at[:, pl.ds(start, width)], full.at[half, rows, pl.ds(place, width)], sem
                    )
                )
    for copy in copies:
        copy.start()
    return copies


def shards(ref, first=0):
    return [ref.at[pl.ds(SHARD * (first + step), SHARD)] for step in range(8)]


def load_space(ids, refs, full, sem):
    finish(load(ids, [(shards(refs[0]), shards(refs[1]), 0, HALF_D, 0)], full, sem))


def load_time(ids, refs, full, sem):
    def place(step):
        return pl.multiple_of(((ids[2] + step) & 1) * PART, 128)

    parts = [(refs[:4], refs[4:8], 0, REST, 2 * PART)]
    parts += [(shards(refs[8 + s]), shards(refs[10], 8 * s), 0, PART, place(s)) for s in range(2)]
    return load(ids, parts, full, sem)


def finish(copies):
    for copy in copies:
        copy.wait()


def interleave(first, second):
    parts = [part.astype(F32).reshape(32, 8, D) for part in (first, second)]
    return jnp.concatenate(parts, axis=1).astype(BF)


def project_first(ids, *refs):
    mix, residual, out, full, sem = refs[2:]
    load_space(ids, refs, full, sem)
    project(mix, full, residual, out)


def time_block(ids, *refs):
    hidden, cot, bias, gain, mix, grad_cols, sent, gain_term, full, qkv, probs, out, grad, acc, sem = refs[11:]
    copies = load_time(ids, refs, full, sem)
    standard, _ = standardise(hidden)
    normed = (standard * gain[...]).astype(BF)
    finish(copies)

    qkv[:, :HALF_TIME] = nn(normed, full[0]).astype(BF)
    qkv[:, HALF_TIME:] = nn(normed, full[1, :, :D]).astype(BF)
    attend(qkv, probs, acc, bias)
    mix[...] = acc[:, :D].astype(BF)
    out[...] = (hidden[...].astype(F32) + nn(mix[...], full[1, :, D:])).astype(BF)

    grad[...] = nt(cot[...], full[1, :, D:]).astype(BF)
    attend_back(qkv, probs, grad, acc)
    low = acc[...].astype(BF)
    grad_normed = nt(low[:, :HALF_TIME], full[0]) + nt(low[:, HALF_TIME:], full[1, :, :D])
    standard, inv_dev = standardise(hidden)
    scaled = grad_normed * gain[...]
    correction = (
        scaled
        - jnp.mean(scaled, axis=-1, keepdims=True)
        - standard * jnp.mean(scaled * standard, axis=-1, keepdims=True)
    )
    grad_in = cot[...].astype(F32) + correction * inv_dev
    grad_cols[...] = grad_in.astype(BF)
    sent[...] = interleave(grad_in, out[...])
    gain_term[...] = jnp.sum(grad_normed * standard, axis=0, keepdims=True)


def space_backward(ids, *refs):
    qkv, probs, grad_in, out, full, grad, acc, sem = refs[2:]
    load_space(ids, refs, full, sem)
    grad[...] = back_project(grad_in, full).astype(BF)
    attend_back(qkv, probs, grad, acc)
    out[...] = acc[...].astype(BF)


def choose_columns(ids, chosen):
    row = lax.broadcasted_iota(jnp.int32, (D, D // 2), 0)
    col = lax.broadcasted_iota(jnp.int32, (D, D // 2), 1)
    group = lax.shift_right_logical(col * 1821, 16)
    chosen[...] = jnp.where(row == col + 36 * (group + ids[1]), 1.0, 0.0).astype(BF)


def transposed_term(chosen, left, left_other, right, right_other):
    mine = nn(right[...], chosen[...]).astype(BF)
    other = nn(right_other[...], chosen[...]).astype(BF)
    return tn(mine, left[...]) + tn(other, left_other[...])


def both_terms(ids, *refs):
    gain, chosen, outs, cut = refs[8], refs[9], refs[10:14], refs[14]
    for index in range(2):
        term = transposed_term(chosen, *refs[4 * index : 4 * index + 4])
        for y in range(4):
            cols = [term[144 * x : 144 * x + 144, 288 * y : 288 * y + 288] for x in range(4)]
            cut[y, 144 * index : 144 * index + 144] = jnp.concatenate(cols, axis=1)
    cut[:, 288:] = jnp.broadcast_to(gain[...], (4, 16, D))
    for step in range(4):
        outs[step][...] = cut[(ids[0] + step) & 3].astype(BF)


def add_first(*refs):
    out = refs[4]
    total = sum(ref[...].astype(F32) for ref in refs[:4])
    gain = jnp.concatenate([total[288:289, 288 * part : 288 * part + 288] for part in range(4)], axis=0)
    for x in range(4):
        for zh in range(4):
            for zl in range(2):
                lanes = slice(288 * x + 144 * zl, 288 * x + 144 * zl + 144)
                terms = [total[144 * i + 36 * zh : 144 * i + 36 * zh + 36, lanes] for i in range(2)]
                piece = jnp.concatenate([jnp.concatenate(terms, axis=1), gain], axis=0)
                groups = [piece[8 * g : 8 * g + 8] for g in range(5)]
                piece = jnp.concatenate(groups + [jnp.zeros((8, 96), F32)], axis=1)
                out[8 * x + 2 * zh + zl] = piece.astype(BF)


def add_last(got, out):
    total = jnp.sum(got[...].astype(F32), axis=0)
    out[...] = jnp.concatenate([total[:, 288 * g : 288 * g + 288] for g in range(5)], axis=0)


def call(kernel, outs, scratch, *args, us, mib, smem=0, hbm=0):
    specs = [pl.BlockSpec(memory_space=pltpu.SMEM)] * smem
    specs += [pl.BlockSpec(memory_space=pl.ANY)] * hbm
    specs += [VMEM] * (len(args) - smem - hbm)
    return pl.pallas_call(
        kernel,
        out_shape=tuple(jax.ShapeDtypeStruct(s, t) for s, t in outs),
        in_specs=specs,
        out_specs=(VMEM,) * len(outs),
        scratch_shapes=scratch,
        cost_estimate=pl.CostEstimate(
            flops=us * 10**9, bytes_accessed=us * 3 * 10**6, transcendentals=0
        ),
        compiler_params=pltpu.CompilerParams(vmem_limit_bytes=mib * 2**20),
    )(*args)


def exchange(rows, axes):
    return lax.all_to_all(rows, axes, split_axis=0, concat_axis=0, tiled=True)


def swap(value):
    return lax.ppermute(value, "core", [(0, 1), (1, 0)])


def half_of(shard, half, core):
    return lax.dynamic_slice(shard, (0, core * (shard.shape[1] - half)), (SHARD, half))


def pair_up(piece, zl):
    other = lax.ppermute(piece, "zl", [(0, 1), (1, 0)])
    return jnp.where(zl == 0, jnp.concatenate([piece, other]), jnp.concatenate([other, piece]))


def shift(value, axis, step):
    return lax.ppermute(value, axis, [(i, (i + step) % 4) for i in range(4)])


def around(value, axis):
    return [shift(value, axis, step) for step in range(1, 4)]


def deal(pieces, axis):
    return [shift(pieces[step], axis, step) for step in range(1, 4)]


def body(block_in, spatial_qkv, cotangent, w_sproj, w_tqkv, w_tproj, t_gain):
    core, x, y, zl = (lax.axis_index(name) for name in ("core", "x", "y", "zl"))
    ids = jnp.stack([y, core, x, zl]).astype(jnp.int32)
    block_rows = block_in.reshape(TOK, D)
    qkv = spatial_qkv.reshape(TOK, 3 * D)
    gain = t_gain.reshape(1, D)
    rows_shape = ((TOK, D), BF)
    wide_shape = ((TOK, 3 * D), BF)
    both_shape = ((32, 16, D), BF)
    probs_shape = ((HEADS, TOK, TOK), BF)
    sem = pltpu.SemaphoreType.DMA
    full_space = pltpu.VMEM((2, D, HALF_D), BF)
    full_time = pltpu.VMEM((2, D, HALF_TIME), BF)
    rows_acc = pltpu.VMEM((TOK, D), F32)
    wide_acc = pltpu.VMEM((TOK, 3 * D), F32)
    rows_low = pltpu.VMEM((TOK, D), BF)
    wide_low = pltpu.VMEM((TOK, 3 * D), BF)
    probs_low = pltpu.VMEM(*probs_shape)

    time_half = jnp.where(
        core == 0, w_tqkv[:, :HALF_TIME], jnp.concatenate([w_tqkv[:, HALF_TIME:], w_tproj], axis=1)
    )
    part = lax.dynamic_slice(time_half, (0, PART * (x % 2)), (SHARD, PART))
    first = jnp.concatenate([half_of(w_sproj, HALF_D, core), part], axis=1)
    rest = time_half[:, 2 * PART :]
    space_mix, space_probs = call(
        space_forward, (rows_shape, probs_shape), [rows_acc], qkv, us=40, mib=20
    )
    other, rest, space_mix, cotangent, *own = lax.optimization_barrier(
        (lax.ppermute(first, "zl", [(0, 1), (1, 0)]), rest, space_mix, cotangent, first, *around(first, "y"))
    )
    rest_pair, *arrived = lax.optimization_barrier((pair_up(rest, zl), *own, other, *around(other, "y")))
    space_mine = jnp.concatenate([piece[:, :HALF_D] for piece in arrived])
    part_mine = jnp.concatenate([piece[:, HALF_D:] for piece in arrived])
    cot_cols, space_mix, space_mine, space_theirs = lax.optimization_barrier(
        (exchange(cotangent.reshape(TOK, D), SEQ), space_mix, space_mine, swap(space_mine))
    )
    (hidden,) = call(
        project_first,
        (rows_shape,),
        [full_space, sem],
        ids, space_mine, space_theirs, space_mix, block_rows,
        us=60, mib=60, smem=1, hbm=2,
    )
    hidden, late_ids = lax.optimization_barrier((hidden, ids))
    (chosen,) = call(choose_columns, (((D, D // 2), BF),), [], late_ids, us=100, mib=60, smem=1)
    (bias,) = call(same_patch, (((TOK, TOK), F32),), [], late_ids, us=100, mib=60, smem=1)
    hidden_cols, bias, chosen, space_mix, own_theirs, part_other, *rest_mine = lax.optimization_barrier(
        (
            exchange(hidden, SEQ), bias, chosen, space_mix, swap(rest_pair),
            lax.ppermute(part_mine, "x", [(i, i ^ 1) for i in range(4)]), rest_pair, *around(rest_pair, "y"),
        )
    )
    time_weights = [*rest_mine, own_theirs, *[swap(pair) for pair in rest_mine[1:]]]
    time_weights += [part_mine, part_other, swap(jnp.concatenate([part_mine, part_other]))]

    time_mix, grad_cols, sent, gain_term = call(
        time_block,
        (rows_shape, rows_shape, both_shape, ((1, D), F32)),
        [full_time, wide_low, probs_low, rows_low, rows_low, wide_acc, sem],
        ids, *time_weights, hidden_cols, cot_cols, bias, gain,
        us=60, mib=60, smem=1, hbm=11,
    )
    mix_cols, time_mix, cot_cols, grad_cols, sent, gain_term = lax.optimization_barrier(
        (exchange(space_mix, SEQ), time_mix, cot_cols, grad_cols, sent, gain_term)
    )
    terms = call(
        both_terms,
        (((304, D), BF),) * 4,
        [pltpu.VMEM((4, 304, D), F32)],
        ids,
        mix_cols, swap(mix_cols), grad_cols, swap(grad_cols),
        time_mix, swap(time_mix), cot_cols, swap(cot_cols),
        gain_term + swap(gain_term), chosen,
        us=60, mib=40, smem=1,
    )
    (pieces,) = call(add_first, (((32, 8, 1536), BF),), [], terms[0], *deal(terms, "y"), us=3, mib=24)
    pieces, got = lax.optimization_barrier((pieces, exchange(sent, SEQ)))
    grad_in = got[:, :8].reshape(TOK, D)
    block_out = got[:, 8:]
    (grad_qkv,) = call(
        space_backward,
        (wide_shape,),
        [full_space, rows_low, wide_acc, sem],
        ids, space_mine, space_theirs, qkv, space_probs, grad_in,
        us=60, mib=60, smem=1, hbm=2,
    )
    last, grad_qkv = lax.optimization_barrier((exchange(pieces, ("x", "zh", "zl")), grad_qkv))
    (last,) = call(add_last, (((40, 288), F32),), [], last, us=1, mib=12)

    shape = block_in.shape
    return (
        block_out.reshape(shape),
        grad_in.reshape(shape),
        grad_qkv.reshape(spatial_qkv.shape),
        last[:36, :144].T,
        last[:36, 144:].T,
        last[36:].reshape(D),
    )


def solution(mesh):
    fine = Mesh(mesh.devices.reshape(4, 4, 2, 4, 2), ("x", "zh", "core", "y", "zl"))
    tokens = P(FS, SEQ, None, None)
    weights = P(FS, None)
    return jax.shard_map(
        body,
        mesh=fine,
        in_specs=(tokens, tokens, tokens, weights, weights, weights, P()),
        out_specs=(tokens, tokens, tokens, P(FS, SEQ), P(FS, SEQ), P()),
        check_vma=False,
    )
```
